128 devices in a mesh: ctx: 32 (over y, x, core), head: 4 (over z).
Axes of the slice: x: 4, y: 4, z: 4, core: 2. Of those that a mesh axis runs over, the one named last changes fastest.
Arguments:
- inputs: bfloat16 [16384, 4096], P('ctx'), may hold values from -8 to 8
- query_weight: bfloat16 [4096, 2048], P(None, 'head'), may hold values from -0.09375 to 0.09375
- key_weight: bfloat16 [4096, 512], P(None, 'head'), may hold values from -0.09375 to 0.09375
- value_weight: bfloat16 [4096, 512], P(None, 'head'), may hold values from -0.09375 to 0.09375
- out_grad: bfloat16 [16384, 2048], P('ctx', 'head'), may hold values from -6 to 6
- doc_lengths: int32 [32], replicated, may hold values from 128 to 1536, as said below
Outputs:
- attn_out: bfloat16 [16384, 2048], P('ctx', 'head')
- input_grad: bfloat16 [16384, 4096], P('ctx', 'head')
- query_weight_grad: float32 [4096, 2048], P('ctx', 'head')
- key_weight_grad: float32 [4096, 512], P('ctx', 'head')
- value_weight_grad: float32 [4096, 512], P('ctx', 'head')
The draws below stay inside these ranges and needn't reach their ends.
Inputs may be any that keep to these rules, and one draw needn't show every extreme that they name: `doc_lengths`: each length is a positive multiple of 128; the lengths sum to 16384; the largest is exactly 1536.
All inputs are finite; a program needn't handle non-finite values.
Results may differ from the reference program's by a relative error of at most 0.018.
The reference program's roundings to bfloat16 on the way count: a program that leaves them out, or rounds other values in their place, can miss the bound.
Values may be sent and summed in bfloat16 or wider, within the bound.
A program may use at most 128 MiB of HBM per device.

```python
import jax
import jax.numpy as jnp
from jax import lax

D = 4096
HD = 128
GROUP = 4
KV_DEV = 1
TOK_DEV = 512
GRAIN = 128
SPAN = 3
KVH = 4
HEADS = 16
TOKENS = 16384
MAXDOC = 1536
NDOCS = 32
N_CTX = 32
N_HEAD = 4


def draw_inputs(key, part):
    base_key, scale_key = jax.random.split(jax.random.fold_in(key, 11))
    base = jax.random.truncated_normal(base_key, -4.0, 4.0, (TOKENS, D), jnp.float32)
    row_scale = jnp.exp(jax.random.uniform(scale_key, (TOKENS, 1), jnp.float32, jnp.log(0.5), jnp.log(2.0)))
    return (base * row_scale).astype(jnp.bfloat16)


def draw_doc_lengths(key, part):
    grain_total = TOKENS // GRAIN
    most_grains = MAXDOC // GRAIN
    other_docs = NDOCS - 1
    extra_grains = grain_total - most_grains - other_docs
    pick_key, place_key, order_key = jax.random.split(jax.random.fold_in(key, 23), 3)
    picks_one = jax.random.randint(jax.random.fold_in(pick_key, 1), (extra_grains,), 0, other_docs)
    picks_two = jax.random.randint(jax.random.fold_in(pick_key, 2), (extra_grains,), 0, other_docs)
    picks = jnp.minimum(picks_one, picks_two).astype(jnp.int32)

    def add_one(step_idx, counts):
        target = picks[step_idx]
        has_room = counts < most_grains - 1
        fallback = jnp.argmax(has_room.astype(jnp.int32)).astype(jnp.int32)
        chosen = jnp.where(has_room[target], target, fallback)
        return counts.at[chosen].add(1)
    counts = lax.fori_loop(0, extra_grains, add_one, jnp.zeros((other_docs,), jnp.int32))
    counts = jax.random.permutation(order_key, counts + 1)
    spot = jax.random.randint(place_key, (), 0, NDOCS).astype(jnp.int32)
    index_all = jnp.arange(NDOCS, dtype=jnp.int32)
    before = counts[jnp.clip(index_all, 0, other_docs - 1)]
    after = counts[jnp.clip(index_all - 1, 0, other_docs - 1)]
    grains = jnp.where(index_all < spot, before, jnp.where(index_all == spot, most_grains, after))
    return (grains * GRAIN).astype(jnp.int32)


def block_scale(stream_key, shape, pieces, smallest, high):
    factor_of = 1.0
    for position, blocks in pieces:
        heights = jax.random.uniform(jax.random.fold_in(jax.random.fold_in(stream_key, 6), position), (blocks,), jnp.float32, smallest / len(pieces), high / len(pieces))
        factor_of = factor_of * jnp.repeat(jnp.exp(heights), shape[position] // blocks).reshape((-1,) + (1,) * (len(shape) - 1 - position))
    return factor_of


def gaussian(stream_key, extent, scale, limit, cuts=(), kind=jnp.bfloat16):
    values = jax.random.normal(stream_key, extent, jnp.float32) * scale
    if len(cuts) > 0:
        values = block_scale(stream_key, extent, cuts, -0.22, 0.18) * values
    return jnp.clip(values, min=-limit, max=limit).astype(kind)


def setup_inputs(seed: int = 0) -> dict:
    seeds = jax.random.split(jax.random.key(seed), 7)
    return {
        "inputs": draw_inputs(jax.random.fold_in(seeds[6], 71), 0),
        "query_weight": gaussian(seeds[1], (D, HEADS * HD), D ** -0.5, 0.09375, ((1, 4),)),
        "key_weight": gaussian(seeds[2], (D, KVH * HD), D ** -0.5, 0.09375, ((1, 4),)),
        "value_weight": gaussian(seeds[3], (D, KVH * HD), D ** -0.5, 0.09375, ((1, 4),)),
        "out_grad": gaussian(seeds[4], (TOKENS, HEADS * HD), 1.0, 6.0, ((0, 32), (1, 4))),
        "doc_lengths": draw_doc_lengths(jax.random.fold_in(seeds[6], 71), 0),
    }


NEG = -1.0e30


def visible(query_pos, query_start, key_pos):
    return (key_pos[None, :] >= query_start[:, None]) & (key_pos[None, :] <= query_pos[:, None])


def block_scores(query_blk, key_blk):
    return jnp.einsum("qkgd,skd->kgqs", query_blk.astype(jnp.float32), key_blk.astype(jnp.float32)) * (HD ** -0.5)


def take_rows(array, start, count):
    return lax.dynamic_slice_in_dim(array, start, count, 0)


def keep_carry(carry, *others):
    return carry


def stats_live(carry, query_blk, key_blk, mask):
    run_top, run_total = carry
    score = jnp.where(mask, block_scores(query_blk, key_blk), NEG)
    new_top = jnp.maximum(run_top, jnp.max(score, axis=-1))
    weight = jnp.where(mask, jnp.exp(score - new_top[..., None]), 0.0)
    return new_top, run_total * jnp.exp(run_top - new_top) + jnp.sum(weight, axis=-1)


def output_live(accum, query_blk, key_blk, value_blk, mask, lse_blk):
    prob = jnp.where(mask, jnp.exp(block_scores(query_blk, key_blk) - lse_blk[..., None]), 0.0)
    prob_low = lax.optimization_barrier(prob.astype(jnp.bfloat16)).astype(jnp.float32)
    return accum + jnp.einsum("kgqs,skd->qkgd", prob_low, value_blk.astype(jnp.float32))


def grads_live(carry, query_blk, key_blk, value_blk, grad_blk, mask, lse_blk, delta_blk, key_at):
    query_acc, key_acc, value_acc = carry
    scale = HD ** -0.5
    prob = jnp.where(mask, jnp.exp(block_scores(query_blk, key_blk) - lse_blk[..., None]), 0.0)
    prob_low = lax.optimization_barrier(prob.astype(jnp.bfloat16)).astype(jnp.float32)
    grad_f = grad_blk.astype(jnp.float32)
    dprob = jnp.einsum("qkgd,skd->kgqs", grad_f, value_blk.astype(jnp.float32))
    dscore = lax.optimization_barrier((prob * (dprob - delta_blk[..., None])).astype(jnp.bfloat16)).astype(jnp.float32)
    query_acc = query_acc + scale * jnp.einsum("kgqs,skd->qkgd", dscore, key_blk.astype(jnp.float32))
    key_part = scale * jnp.einsum("kgqs,qkgd->skd", dscore, query_blk.astype(jnp.float32))
    value_part = jnp.einsum("kgqs,qkgd->skd", prob_low, grad_f)
    key_acc = lax.dynamic_update_slice_in_dim(key_acc, take_rows(key_acc, key_at, TOK_DEV) + key_part, key_at, 0)
    value_acc = lax.dynamic_update_slice_in_dim(value_acc, take_rows(value_acc, key_at, TOK_DEV) + value_part, key_at, 0)
    return query_acc, key_acc, value_acc


def dot_nt(left_mat, right_mat):
    return lax.dot_general(left_mat, right_mat, (((1,), (1,)), ((), ())), preferred_element_type=jnp.float32)


def reference(inputs, query_weight, key_weight, value_weight, out_grad, doc_lengths):
    n_tok = inputs.shape[0]
    kv_heads = KV_DEV * N_HEAD
    query = lax.optimization_barrier(jnp.dot(inputs, query_weight, preferred_element_type=jnp.float32).astype(jnp.bfloat16))
    keys_all = lax.optimization_barrier(jnp.dot(inputs, key_weight, preferred_element_type=jnp.float32).astype(jnp.bfloat16))
    values_all = lax.optimization_barrier(jnp.dot(inputs, value_weight, preferred_element_type=jnp.float32).astype(jnp.bfloat16))
    query4 = query.reshape(n_tok, kv_heads, GROUP, HD)
    keys3 = keys_all.reshape(n_tok, kv_heads, HD)
    values3 = values_all.reshape(n_tok, kv_heads, HD)
    positions = jnp.arange(n_tok, dtype=jnp.int32)
    doc_ends = jnp.cumsum(doc_lengths).astype(jnp.int32)
    starts = jnp.sum(jnp.where(doc_ends[None, :] <= positions[:, None], doc_lengths[None, :], 0), axis=1).astype(jnp.int32)
    local_pos = jnp.arange(TOK_DEV, dtype=jnp.int32)

    def forward_shard(shard):
        first = shard * TOK_DEV
        query_blk = take_rows(query4, first, TOK_DEV)
        query_pos = first + local_pos
        query_start = take_rows(starts, first, TOK_DEV)
        carry = (jnp.full((kv_heads, GROUP, TOK_DEV), NEG, jnp.float32), jnp.zeros((kv_heads, GROUP, TOK_DEV), jnp.float32))
        for distance in range(SPAN + 1):
            key_first = (shard - distance) * TOK_DEV
            mask = visible(query_pos, query_start, key_first + local_pos)
            key_blk = take_rows(keys3, jnp.maximum(key_first, 0), TOK_DEV)
            carry = lax.cond(jnp.any(mask), stats_live, keep_carry, carry, query_blk, key_blk, mask)
        lse_blk = carry[0] + jnp.log(carry[1])
        accum = jnp.zeros((TOK_DEV, kv_heads, GROUP, HD), jnp.float32)
        for distance in range(SPAN + 1):
            key_first = (shard - distance) * TOK_DEV
            mask = visible(query_pos, query_start, key_first + local_pos)
            key_at = jnp.maximum(key_first, 0)
            accum = lax.cond(jnp.any(mask), output_live, keep_carry, accum, query_blk,
                             take_rows(keys3, key_at, TOK_DEV), take_rows(values3, key_at, TOK_DEV), mask, lse_blk)
        return lax.optimization_barrier(accum.astype(jnp.bfloat16)), lse_blk

    outs, lse_all = lax.map(forward_shard, jnp.arange(N_CTX, dtype=jnp.int32))
    attn4 = outs.reshape(n_tok, kv_heads, GROUP, HD)
    attn_out = attn4.reshape(n_tok, kv_heads * GROUP * HD)
    grad4 = out_grad.reshape(n_tok, kv_heads, GROUP, HD)
    delta_all = jnp.sum(grad4.astype(jnp.float32) * attn4.astype(jnp.float32), axis=-1)

    def backward_shard(carry, shard):
        key_acc, value_acc = carry
        first = shard * TOK_DEV
        query_blk = take_rows(query4, first, TOK_DEV)
        grad_blk = take_rows(grad4, first, TOK_DEV)
        query_pos = first + local_pos
        query_start = take_rows(starts, first, TOK_DEV)
        lse_blk = lax.dynamic_index_in_dim(lse_all, shard, 0, keepdims=False)
        delta_blk = jnp.transpose(take_rows(delta_all, first, TOK_DEV), (1, 2, 0))
        state = (jnp.zeros((TOK_DEV, kv_heads, GROUP, HD), jnp.float32), key_acc, value_acc)
        for distance in range(SPAN + 1):
            key_first = (shard - distance) * TOK_DEV
            mask = visible(query_pos, query_start, key_first + local_pos)
            key_at = jnp.maximum(key_first, 0)
            state = lax.cond(jnp.any(mask), grads_live, keep_carry, state, query_blk,
                             take_rows(keys3, key_at, TOK_DEV), take_rows(values3, key_at, TOK_DEV),
                             grad_blk, mask, lse_blk, delta_blk, key_at)
        return (state[1], state[2]), state[0]

    zero_kv = jnp.zeros((n_tok, kv_heads, HD), jnp.float32)
    (key_acc, value_acc), query_grads = lax.scan(backward_shard, (zero_kv, zero_kv), jnp.arange(N_CTX, dtype=jnp.int32))
    dq_low = lax.optimization_barrier(query_grads.reshape(n_tok, kv_heads * GROUP * HD).astype(jnp.bfloat16))
    dk_low = lax.optimization_barrier(key_acc.reshape(n_tok, kv_heads * HD).astype(jnp.bfloat16))
    dv_low = lax.optimization_barrier(value_acc.reshape(n_tok, kv_heads * HD).astype(jnp.bfloat16))
    q_cols = GROUP * KV_DEV * HD
    k_cols = KV_DEV * HD
    total_grad = jnp.zeros((n_tok, inputs.shape[1]), jnp.float32)
    for group_idx in range(N_HEAD):
        qa, qb = group_idx * q_cols, (group_idx + 1) * q_cols
        ka, kb = group_idx * k_cols, (group_idx + 1) * k_cols
        piece = dot_nt(dq_low[:, qa:qb], query_weight[:, qa:qb]) + dot_nt(dk_low[:, ka:kb], key_weight[:, ka:kb]) + dot_nt(dv_low[:, ka:kb], value_weight[:, ka:kb])
        total_grad = total_grad + lax.optimization_barrier(piece.astype(jnp.bfloat16)).astype(jnp.float32)
    input_grad = total_grad.astype(jnp.bfloat16)
    joined = jnp.concatenate([dq_low, dk_low, dv_low], axis=1)
    weight_grad = lax.dot_general(inputs, joined, (((0,), (0,)), ((), ())), preferred_element_type=jnp.float32)
    all_q = kv_heads * GROUP * HD
    all_k = kv_heads * HD
    return (attn_out, input_grad, weight_grad[:, :all_q], weight_grad[:, all_q:all_q + all_k], weight_grad[:, all_q + all_k:])
```

```python
import functools
import math

import jax
import jax.numpy as jnp
from jax import lax
from jax.experimental import pallas as pl
from jax.experimental.pallas import tpu as pltpu
from jax.sharding import PartitionSpec as P

HD = 128
GROUP = 4
TOK = 512
D = 4096
QB = 256
WIN = 1664
COLS = 768
NEG = -1e30
MESH = pl.DeviceIdType.MESH
F32 = jnp.float32
BF16 = jnp.bfloat16

NN = (((1,), (0,)), ((), ()))
NT = (((1,), (1,)), ((), ()))


def dot(a, b, dims=NN):
    return lax.dot_general(a, b, dims, preferred_element_type=F32)


class Copies:
    def __init__(self, send_sem, recv_sem):
        self.send_sem, self.recv_sem, self.used = send_sem, recv_sem, 0
        self.sent = []

    def make(self, src, dst, device):
        idx = self.used
        self.used += 1
        return pltpu.make_async_remote_copy(
            src_ref=src,
            dst_ref=dst,
            send_sem=self.send_sem.at[idx],
            recv_sem=self.recv_sem.at[idx],
            device_id=device,
            device_id_type=MESH,
        )

    def start(self, src, dst, device):
        copy = self.make(src, dst, device)
        copy.start()
        self.sent.append(copy)
        return copy


N_COPIES = 80


def kernel(
    doc_ref, x_hbm, wq_hbm, wk_hbm, wv_hbm, do_hbm,
    out_ref, ig_ref, wqg_ref, wkg_ref, wvg_ref,
    x_v, w_v, do_v, kv, kT, vT, q_h, doT, acc, bias, xT, xTs, wz, joined, joined_s, jz,
    dkv_send, dkv_sib, dkv_x, r2p, r2m, r1p, r1m, s2, sp, sm, t_f, u2p, u2m, u1p, u1m, t2, tp, tm,
    ig_acc, send_sem, recv_sem, load_sem,
):
    ctx = lax.axis_index("ctx")
    z = lax.axis_index("head")
    chip = ctx // 2
    k = ctx % 2
    y, x = chip // 4, chip % 4
    factor = HD ** -0.5

    def at(yy, xx, kk, zz):
        return ((yy % 4) * 8 + (xx % 4) * 2 + kk, zz % 4)

    def chip_at(pp, kk):
        return ((pp % 16) * 2 + kk, z)

    sib = at(y, x, 1 - k, z)
    z_peer = [None] + [at(y, x, k, z + r) for r in (1, 2, 3)]
    y_peer = [None] + [at(y + r, x, k, z) for r in (1, 2, 3)]
    x_peer = [None] + [at(y, x + r, k, z) for r in (1, 2, 3)]
    nxt, prv = chip_at(chip + 1, k), chip_at(chip + 15, k)
    third = chip_at(jnp.where(k == 1, chip + 2, chip + 14), 1 - k)

    loads = [
        pltpu.make_async_copy(wk_hbm, w_v.at[:, 512:640], load_sem.at[0]),
        pltpu.make_async_copy(wv_hbm, w_v.at[:, 640:768], load_sem.at[1]),
        pltpu.make_async_copy(x_hbm, x_v, load_sem.at[2]),
        pltpu.make_async_copy(wq_hbm, w_v.at[:, 0:512], load_sem.at[3]),
        pltpu.make_async_copy(do_hbm, do_v, load_sem.at[4]),
    ]
    for load in loads:
        load.start()

    barrier = pltpu.get_barrier_semaphore()
    partners = [sib, *z_peer[1:], *y_peer[1:], x_peer[1], x_peer[3], nxt, prv, third]
    for partner in partners:
        pl.semaphore_signal(barrier, inc=1, device_id=partner, device_id_type=MESH)

    copies = Copies(send_sem, recv_sem)

    loads[0].wait()
    loads[1].wait()
    loads[2].wait()
    kv[1536:2048, :] = dot(x_v[...], w_v[:, 512:768]).astype(BF16)
    pl.semaphore_wait(barrier, len(partners))

    own_kv = kv.at[1536:2048]
    kv1 = copies.start(own_kv, kv.at[512:1024], nxt)
    kv2 = copies.make(own_kv, kv.at[1024:1536], sib)
    kv0 = copies.make(own_kv, kv.at[0:512], third)

    @pl.when(k == 0)
    def _():
        kv2.start()

    @pl.when(k == 1)
    def _():
        kv0.start()

    loads[3].wait()
    wz_got = []
    for r in (1, 2, 3):
        rows = pl.multiple_of(((z + r) % 4) * 1024 + y * 256 + k * 128, 128)
        wz_got.append(copies.start(w_v.at[pl.ds(rows, 128), :], wz.at[r - 1, y, k], z_peer[r]))
    for h in range(GROUP):
        if h % 2 == 0:
            both = dot(x_v[...], w_v[:, h * HD : (h + 2) * HD]).astype(BF16)
            q_h[h] = both[:, :HD]
            q_h[h + 1] = both[:, HD:]

    def transpose_x(i, carry):
        own = pl.multiple_of((2 * i + k) * 128, 128)
        other = pl.multiple_of((2 * i + 1 - k) * 128, 128)
        xT[0, i // 4, i % 4] = x_v[:, pl.ds(own, 128)].T
        xT[1, i // 4, i % 4] = x_v[:, pl.ds(other, 128)].T
        return carry

    lax.fori_loop(0, 16, transpose_x, 0)
    x_got = copies.start(xT.at[1], xTs, sib)

    loads[4].wait()
    for h in range(GROUP):
        doT[h] = do_v[:, h * HD : (h + 1) * HD].T

    pos = ctx * TOK + lax.broadcasted_iota(jnp.int32, (1, TOK), 1)
    start = jnp.zeros((1, TOK), jnp.int32)
    end = jnp.int32(0)
    for j in range(32):
        length = doc_ref[j]
        end = end + length
        start = start + jnp.where(pos >= end, length, 0)
    first = start - (ctx - 3) * TOK
    for b in range(2):
        key_pos = 128 + QB * b + lax.broadcasted_iota(jnp.int32, (WIN, QB), 0)
        query_pos = 1536 + QB * b + lax.broadcasted_iota(jnp.int32, (WIN, QB), 1)
        seen = (key_pos >= first[:, b * QB : (b + 1) * QB]) & (key_pos <= query_pos)
        bias[b] = jnp.where(seen, 0.0, NEG)

    wy_got = []
    for got in wz_got:
        got.wait_recv()
    mine = wz.at[:, y, k]
    for r in (1, 2, 3):
        wy_got.append(copies.start(mine, mine, y_peer[r]))

    kv1.wait_recv()
    fwd2 = copies.make(kv.at[512:1024], kv.at[1024:1536], sib)
    fwd0 = copies.make(kv.at[512:1024], kv.at[0:512], sib)

    @pl.when(k == 0)
    def _():
        fwd0.start()
        fwd2.wait_recv()
        kv0.wait_recv()

    @pl.when(k == 1)
    def _():
        fwd2.start()
        kv2.wait_recv()
        fwd0.wait_recv()

    for i in range(4):
        rows = slice(i * 512, (i + 1) * 512)
        kT[:, rows] = kv[rows, 0:HD].T
        vT[:, rows] = kv[rows, HD:].T
    acc[...] = jnp.zeros_like(acc)

    coef = factor * math.log2(math.e)

    def attend(h, b):
        win = pl.ds(pl.multiple_of(128 + QB * b, 128), WIN)
        rows = pl.ds(pl.multiple_of(QB * b, QB), QB)
        cols = pl.ds(h * HD, HD)
        key, value = kv[win, 0:HD], kv[win, HD:]
        q = q_h[h, rows, :]
        do = do_v[rows, cols]
        score = dot(key, q, NT) + bias[b]
        top = jnp.max(score, axis=0, keepdims=True)
        weight = jnp.exp2((score - top) * coef)
        prob = weight * (1.0 / jnp.sum(weight, axis=0, keepdims=True))
        low = prob.astype(BF16)
        o_t = dot(vT[:, win], low).astype(BF16)
        delta = jnp.sum(o_t.astype(F32) * doT[h, :, rows].astype(F32), axis=0, keepdims=True)
        dscore = (prob * (dot(value, do, NT) - delta)).astype(BF16)
        out_ref[rows, cols] = o_t.T
        dq_t = dot(kT[:, win], dscore) * factor
        joined[h // 2, rows, (h % 2) * HD : (h % 2 + 1) * HD] = dq_t.T.astype(BF16)
        acc[win, 0:HD] += dot(dscore, q)
        acc[win, HD:] += dot(low, do)

    def attend_head(h):
        def step(b, carry):
            attend(h, b)
            return carry

        lax.fori_loop(0, 2, step, 0)

    def share(chunk):
        here = joined.at[chunk]
        return (
            copies.start(here, joined_s.at[chunk], sib),
            copies.start(here, jz.at[0, chunk], z_peer[1]),
            copies.start(here, jz.at[2, chunk], z_peer[3]),
        )

    def share_far(chunk, got):
        got[1].wait_recv()
        got[2].wait_recv()
        top, low = slice(0, 256), slice(256, 512)
        return (
            copies.start(jz.at[0, chunk, top], jz.at[1, chunk, top], z_peer[1]),
            copies.start(jz.at[2, chunk, low], jz.at[1, chunk, low], z_peer[3]),
        )

    def lhs(ref, axis, there):
        if axis == "y":
            return ref[there].reshape(512, TOK)
        return ref[:, there].reshape(512, TOK)

    def product(chunk, axis, there):
        full = dot(lhs(xT.at[0], axis, there), joined[chunk])
        full = full + dot(lhs(xTs, axis, there), joined_s[chunk])
        return full.reshape(4, 128, 256)

    axes = {"y": (y, y_peer), "x": (x, x_peer)}
    order = (("y", "x"), ("y", "x"), ("x", "y"))

    def reduce_first(chunk):
        axis = order[chunk][0]
        here, peer = axes[axis]
        s2[chunk] = product(chunk, axis, (here + 2) % 4).astype(BF16)
        return (
            copies.start(s2.at[chunk, 0:2], r2p.at[chunk], peer[1]),
            copies.start(s2.at[chunk, 2:4], r2m.at[chunk], peer[3]),
        )

    def reduce_second(chunk, got):
        axis = order[chunk][0]
        here, peer = axes[axis]
        up = product(chunk, axis, (here + 1) % 4)
        got[0].wait_recv()
        sp[chunk, 0:2] = (up[0:2] + r2p[chunk].astype(F32)).astype(BF16)
        sp[chunk, 2:4] = up[2:4].astype(BF16)
        one = copies.start(sp.at[chunk], r1p.at[chunk], peer[1])
        down = product(chunk, axis, (here + 3) % 4)
        got[1].wait_recv()
        sm[chunk, 0:2] = down[0:2].astype(BF16)
        sm[chunk, 2:4] = (down[2:4] + r2m[chunk].astype(F32)).astype(BF16)
        return one, copies.start(sm.at[chunk], r1m.at[chunk], peer[3])

    def reduce_third(chunk, got):
        axis = order[chunk][0]
        here, _ = axes[axis]
        own = product(chunk, axis, here)
        got[0].wait_recv()
        got[1].wait_recv()
        t_f[chunk] = own + r1p[chunk].astype(F32) + r1m[chunk].astype(F32)
        here, peer = axes[order[chunk][1]]
        t2[chunk] = t_f[chunk, (here + 2) % 4].astype(BF16)
        return (
            copies.start(t2.at[chunk, 0:64], u2p.at[chunk], peer[1]),
            copies.start(t2.at[chunk, 64:128], u2m.at[chunk], peer[3]),
        )

    def reduce_fourth(chunk, got):
        here, peer = axes[order[chunk][1]]
        up = t_f[chunk, (here + 1) % 4]
        got[0].wait_recv()
        tp[chunk, 0:64] = (up[0:64] + u2p[chunk].astype(F32)).astype(BF16)
        tp[chunk, 64:128] = up[64:128].astype(BF16)
        one = copies.start(tp.at[chunk], u1p.at[chunk], peer[1])
        down = t_f[chunk, (here + 3) % 4]
        got[1].wait_recv()
        tm[chunk, 0:64] = down[0:64].astype(BF16)
        tm[chunk, 64:128] = (down[64:128] + u2m[chunk].astype(F32)).astype(BF16)
        return one, copies.start(tm.at[chunk], u1m.at[chunk], peer[3])

    def reduce_last(chunk, got):
        here, _ = axes[order[chunk][1]]
        got[0].wait_recv()
        got[1].wait_recv()
        return t_f[chunk, here] + u1p[chunk].astype(F32) + u1m[chunk].astype(F32)

    def add_own(chunk):
        rows = pl.multiple_of(z * 1024, 1024)
        cols = slice(chunk * 256, (chunk + 1) * 256)
        term = dot(joined[chunk], w_v[pl.ds(rows, 1024), cols], NT)
        if chunk == 0:
            ig_acc[...] = term
        else:
            ig_acc[...] += term

    def add_far(chunk, slot):
        cols = slice(chunk * 256, (chunk + 1) * 256)
        weights = wz[slot, :, :, :, cols].reshape(1024, 256)
        ig_acc[...] += dot(jz[slot, chunk], weights, NT)

    attend_head(0)
    attend_head(1)
    got0 = share(0)
    for got in wy_got:
        got.wait_recv()
    ws_got = copies.start(wz.at[:, :, k], wz.at[:, :, k], sib)
    x_got.wait_recv()

    attend_head(2)
    got0[0].wait_recv()
    ring0 = reduce_first(0)
    far0 = share_far(0, got0)
    attend_head(3)
    got1 = share(1)

    ones = lax.broadcasted_iota(jnp.int32, (1, 2 * HD), 1)
    scale = jnp.where(ones < HD, factor, 1.0)
    dkv_send[0] = (acc[0:512] * scale).astype(BF16)
    dkv_send[1] = (acc[1024:1536] * scale).astype(BF16)
    pair_a = copies.make(dkv_send.at[1], dkv_sib.at[0], sib)
    pair_b = copies.make(dkv_send.at[0], dkv_sib.at[1], sib)
    far_d = copies.make(dkv_send.at[0], dkv_sib.at[1], third)
    pair_a.start()

    @pl.when(k == 1)
    def _():
        pair_b.start()

    @pl.when(k == 0)
    def _():
        far_d.start()

    pair_a.wait_recv()

    @pl.when(k == 0)
    def _():
        pair_b.wait_recv()

    came = dkv_sib[1 - k].astype(F32)
    dkv_send[2] = (acc[512:1024] * scale + came).astype(BF16)
    near_d = copies.start(dkv_send.at[2], dkv_x, prv)

    ring0 = reduce_second(0, ring0)
    got1[0].wait_recv()
    ring1 = reduce_first(1)
    far1 = share_far(1, got1)
    add_own(0)
    add_own(1)
    near_d.wait_recv()

    @pl.when(k == 1)
    def _():
        far_d.wait_recv()

    total = acc[1536:2048] * scale + dkv_x[...].astype(F32)
    joined[2] = (total + dkv_sib[k].astype(F32)).astype(BF16)
    got2 = share(2)
    ring1 = reduce_second(1, ring1)
    got2[0].wait_recv()
    ring2 = reduce_first(2)
    ring0 = reduce_third(0, ring0)
    add_own(2)
    ws_got.wait_recv()
    add_far(0, 0)
    add_far(0, 2)
    far2 = share_far(2, got2)
    ring2 = reduce_second(2, ring2)
    ring0 = reduce_fourth(0, ring0)
    ring1 = reduce_third(1, ring1)
    far0[0].wait_recv()
    far0[1].wait_recv()
    add_far(0, 1)
    add_far(1, 0)
    add_far(1, 2)
    ring1 = reduce_fourth(1, ring1)
    ring2 = reduce_third(2, ring2)
    far1[0].wait_recv()
    far1[1].wait_recv()
    add_far(1, 1)
    add_far(2, 0)
    add_far(2, 2)
    ring2 = reduce_fourth(2, ring2)
    wqg_ref[:, 0:256] = reduce_last(0, ring0)
    wqg_ref[:, 256:512] = reduce_last(1, ring1)
    far2[0].wait_recv()
    far2[1].wait_recv()
    add_far(2, 1)
    ig_ref[...] = ig_acc[...].astype(BF16)
    last = reduce_last(2, ring2)
    wkg_ref[...] = last[:, 0:128]
    wvg_ref[...] = last[:, 128:256]

    for copy in copies.sent:
        copy.wait_send()
    pair_a.wait_send()

    @pl.when(k == 0)
    def _():
        kv2.wait_send()
        fwd0.wait_send()
        far_d.wait_send()

    @pl.when(k == 1)
    def _():
        kv0.wait_send()
        fwd2.wait_send()
        pair_b.wait_send()


def body(inputs, query_weight, key_weight, value_weight, out_grad, doc_lengths):
    any_space = pl.BlockSpec(memory_space=pl.ANY)
    vmem = pl.BlockSpec(memory_space=pltpu.VMEM)
    return pl.pallas_call(
        kernel,
        out_shape=(
            jax.ShapeDtypeStruct((TOK, 512), BF16),
            jax.ShapeDtypeStruct((TOK, 1024), BF16),
            jax.ShapeDtypeStruct((128, 512), F32),
            jax.ShapeDtypeStruct((128, 128), F32),
            jax.ShapeDtypeStruct((128, 128), F32),
        ),
        in_specs=[pl.BlockSpec(memory_space=pltpu.SMEM)] + [any_space] * 5,
        out_specs=(vmem,) * 5,
        scratch_shapes=[
            pltpu.VMEM((TOK, D), BF16),
            pltpu.VMEM((D, COLS), BF16),
            pltpu.VMEM((TOK, 512), BF16),
            pltpu.VMEM((2048, 256), BF16),
            pltpu.VMEM((HD, 2048), BF16),
            pltpu.VMEM((HD, 2048), BF16),
            pltpu.VMEM((GROUP, TOK, HD), BF16),
            pltpu.VMEM((GROUP, HD, TOK), BF16),
            pltpu.VMEM((2048, 256), F32),
            pltpu.VMEM((2, WIN, QB), F32),
            pltpu.VMEM((2, 4, 4, 128, TOK), BF16),
            pltpu.VMEM((4, 4, 128, TOK), BF16),
            pltpu.VMEM((3, 4, 2, 128, COLS), BF16),
            pltpu.VMEM((3, TOK, 256), BF16),
            pltpu.VMEM((3, TOK, 256), BF16),
            pltpu.VMEM((3, 3, TOK, 256), BF16),
            pltpu.VMEM((3, TOK, 256), BF16),
            pltpu.VMEM((2, TOK, 256), BF16),
            pltpu.VMEM((TOK, 256), BF16),
            pltpu.VMEM((3, 2, 128, 256), BF16),
            pltpu.VMEM((3, 2, 128, 256), BF16),
            pltpu.VMEM((3, 4, 128, 256), BF16),
            pltpu.VMEM((3, 4, 128, 256), BF16),
            pltpu.VMEM((3, 4, 128, 256), BF16),
            pltpu.VMEM((3, 4, 128, 256), BF16),
            pltpu.VMEM((3, 4, 128, 256), BF16),
            pltpu.VMEM((3, 4, 128, 256), F32),
            pltpu.VMEM((3, 64, 256), BF16),
            pltpu.VMEM((3, 64, 256), BF16),
            pltpu.VMEM((3, 128, 256), BF16),
            pltpu.VMEM((3, 128, 256), BF16),
            pltpu.VMEM((3, 128, 256), BF16),
            pltpu.VMEM((3, 128, 256), BF16),
            pltpu.VMEM((3, 128, 256), BF16),
            pltpu.VMEM((TOK, 1024), F32),
            pltpu.SemaphoreType.DMA((N_COPIES,)),
            pltpu.SemaphoreType.DMA((N_COPIES,)),
            pltpu.SemaphoreType.DMA((5,)),
        ],
        compiler_params=pltpu.CompilerParams(
            collective_id=0, has_side_effects=True, vmem_limit_bytes=63 * 2**20
        ),
        cost_estimate=pl.CostEstimate(
            flops=2 * 10**10, bytes_accessed=13 * 10**6, transcendentals=4 * 10**6
        ),
        name="attention_layer",
    )(doc_lengths, inputs, query_weight, key_weight, value_weight, out_grad)


def solution(mesh):
    return jax.shard_map(
        body,
        mesh=mesh,
        in_specs=(
            P("ctx", None),
            P(None, "head"),
            P(None, "head"),
            P(None, "head"),
            P("ctx", "head"),
            P(),
        ),
        out_specs=(P("ctx", "head"),) * 5,
        check_vma=False,
    )
```

```python
import functools
import math

import jax
import jax.numpy as jnp
from jax import lax
from jax.experimental import pallas as pl
from jax.experimental.pallas import tpu as pltpu
from jax.sharding import PartitionSpec as P

HD = 128
GROUP = 4
TOK = 512
D = 4096
QB = 256
WIN = 1664
COLS = 768
NEG = -1e30
MESH = pl.DeviceIdType.MESH
F32 = jnp.float32
BF16 = jnp.bfloat16

NN = (((1,), (0,)), ((), ()))
NT = (((1,), (1,)), ((), ()))


def dot(a, b, dims=NN):
    return lax.dot_general(a, b, dims, preferred_element_type=F32)


class Copies:
    def __init__(self, send_sem, recv_sem):
        self.send_sem, self.recv_sem, self.used = send_sem, recv_sem, 0
        self.sent = []

    def make(self, src, dst, device):
        idx = self.used
        self.used += 1
        return pltpu.make_async_remote_copy(
            src_ref=src,
            dst_ref=dst,
            send_sem=self.send_sem.at[idx],
            recv_sem=self.recv_sem.at[idx],
            device_id=device,
            device_id_type=MESH,
        )

    def plan(self, src, dst, device):
        copy = self.make(src, dst, device)
        self.sent.append(copy)
        return copy

    def start(self, src, dst, device):
        copy = self.plan(src, dst, device)
        copy.start()
        return copy


N_COPIES = 100
TILE = 64
RING = 1


def sum_scratch(width, ring):
    half, whole = pltpu.VMEM((2, 128, width), BF16), pltpu.VMEM((4, 128, width), BF16)
    if ring:
        refs = {"r2p": half, "r2m": half, "r1p": whole, "r1m": whole, "s2": whole, "sp": whole, "sm": whole}
    else:
        blocks = pltpu.VMEM((3, 4, 128, width), BF16)
        refs = {"out1": blocks, "in1": blocks}
    rows = pltpu.VMEM((3, 128, width), BF16)
    return refs | {"out2": rows, "in2": rows, "t": pltpu.VMEM((4, 128, width), F32)}


def kernel(
    doc_ref, x_hbm, wq_hbm, wk_hbm, wv_hbm, do_hbm,
    out_ref, ig_ref, wqg_ref, wkg_ref, wvg_ref,
    x_v, w_v, do_v, kv, kT, vT, q_h, doT, acc, bias, xT, xTo, wz, joined, jz,
    dkv_send, dkv_sib, dkv_x, rings, pb, ig_acc, wg_v, s_f, p_f, low, dsc,
    send_sem, recv_sem, load_sem, store_sem,
):
    ctx = lax.axis_index("ctx")
    z = lax.axis_index("head")
    chip = ctx // 2
    k = ctx % 2
    y, x = chip // 4, chip % 4
    factor = HD ** -0.5

    def at(yy, xx, kk, zz):
        return ((yy % 4) * 8 + (xx % 4) * 2 + kk, zz % 4)

    def chip_at(pp, kk):
        return ((pp % 16) * 2 + kk, z)

    sib = at(y, x, 1 - k, z)
    z_peer = [None] + [at(y, x, k, z + r) for r in (1, 2, 3)]
    y_peer = [None] + [at(y + r, x, k, z) for r in (1, 2, 3)]
    x_peer = [None] + [at(y, x + r, k, z) for r in (1, 2, 3)]
    nxt, prv = chip_at(chip + 1, k), chip_at(chip + 15, k)
    third = chip_at(jnp.where(k == 1, chip + 2, chip + 14), 1 - k)

    loads = [
        pltpu.make_async_copy(wk_hbm, w_v.at[:, 512:640], load_sem.at[0]),
        pltpu.make_async_copy(wv_hbm, w_v.at[:, 640:768], load_sem.at[1]),
        pltpu.make_async_copy(x_hbm, x_v, load_sem.at[2]),
        pltpu.make_async_copy(wq_hbm, w_v.at[:, 0:512], load_sem.at[3]),
        pltpu.make_async_copy(do_hbm, do_v, load_sem.at[4]),
    ]
    for load in loads:
        load.start()

    barrier = pltpu.get_barrier_semaphore()
    partners = [sib, *z_peer[1:], *y_peer[1:], *x_peer[1:], nxt, prv, third]
    for partner in partners:
        pl.semaphore_signal(barrier, inc=1, device_id=partner, device_id_type=MESH)

    ig_v, out_v = x_v.at[:, 0:1024], x_v.at[:, 1024:1536]
    copies = Copies(send_sem, recv_sem)
    stores = []

    def store(src, dst):
        move = pltpu.make_async_copy(src, dst, store_sem.at[len(stores)])
        move.start()
        stores.append(move)

    for load in loads[:3]:
        load.wait()
    kv[1536:2048, :] = dot(x_v[...], w_v[:, 512:768]).astype(BF16)
    pl.semaphore_wait(barrier, len(partners))
    own_kv = kv.at[1536:2048]
    kv1 = copies.start(own_kv, kv.at[512:1024], nxt)
    kv2 = copies.make(own_kv, kv.at[1024:1536], sib)
    kv0a = copies.make(kv.at[1920:2048], kv.at[384:512], third)
    kv0b = copies.make(kv.at[1664:1920], kv.at[128:384], third)

    @pl.when(k == 0)
    def _():
        kv2.start()

    @pl.when(k == 1)
    def _():
        kv0a.start()

    def begin(*group):
        for copy in group:
            copy.start()

    def arrive(*group):
        for copy in group:
            copy.wait_recv()

    for load in loads[3:]:
        load.wait()

    wz_got = []
    for r in (1, 2, 3):
        for begins, rows, part in ((0, 32, y), (32, 96, x)):
            first_row = pl.multiple_of(((z + r) % 4) * 1024 + part * 256 + k * 128 + begins, 32)
            there = wz.at[r - 1, part, k, begins : begins + rows]
            wz_got.append(copies.start(w_v.at[pl.ds(first_row, rows), :], there, z_peer[r]))

    for h in range(0, GROUP, 2):
        both = dot(x_v[...], w_v[:, h * HD : (h + 2) * HD]).astype(BF16)
        q_h[h] = both[:, :HD]
        q_h[h + 1] = both[:, HD:]

    def transpose_x(i, carry):
        own = pl.multiple_of((2 * i + k) * 128, 128)
        other = pl.multiple_of((2 * i + 1 - k) * 128, 128)
        xT[i, :, 0:TOK] = x_v[:, pl.ds(own, 128)].T
        xTo[i] = x_v[:, pl.ds(other, 128)].T
        return carry

    lax.fori_loop(0, 16, transpose_x, 0)
    x_got = copies.start(xTo, xT.at[:, :, TOK : 2 * TOK], sib)

    for h in range(GROUP):
        doT[h] = do_v[:, h * HD : (h + 1) * HD].T

    pos = ctx * TOK + lax.broadcasted_iota(jnp.int32, (1, TOK), 1)
    start = jnp.zeros((1, TOK), jnp.int32)
    end = jnp.int32(0)
    for j in range(32):
        length = doc_ref[j]
        end = end + length
        start = start + jnp.where(pos >= end, length, 0)
    first = start - (ctx - 3) * TOK
    for b in range(2):
        key_pos = 128 + QB * b + lax.broadcasted_iota(jnp.int32, (WIN, QB), 0)
        query_pos = 1536 + QB * b + lax.broadcasted_iota(jnp.int32, (WIN, QB), 1)
        seen = (key_pos >= first[:, b * QB : (b + 1) * QB]) & (key_pos <= query_pos)
        bias[b] = jnp.where(seen, 0.0, NEG)
    acc[...] = jnp.zeros_like(acc)
    dkv_sib[1, 0:128] = jnp.zeros((128, 256), BF16)

    def transpose_kv(begin, stop):
        kT[:, begin:stop] = kv[begin:stop, 0:HD].T
        vT[:, begin:stop] = kv[begin:stop, HD:].T

    transpose_kv(1536, 2048)
    kv1.wait_recv()
    fwd2 = copies.make(kv.at[512:1024], kv.at[1024:1536], sib)
    fwd0 = copies.make(kv.at[640:1024], kv.at[128:512], sib)

    @pl.when(k == 0)
    def _():
        fwd0.start()

    @pl.when(k == 1)
    def _():
        fwd2.start()
        kv0b.start()

    transpose_kv(512, 1024)

    arrive(*wz_got)
    mine_y, mine_x = wz.at[:, y, k, 0:32], wz.at[:, x, k, 32:128]
    wy_got = [copies.start(mine_y, mine_y, y_peer[r]) for r in (1, 2, 3)]
    wx_got = [copies.start(mine_x, mine_x, x_peer[r]) for r in (1, 3)]
    left, right = wz.at[:, (x + 3) % 4, k, 32:80], wz.at[:, (x + 1) % 4, k, 80:128]
    wx_far = (copies.plan(left, left, x_peer[1]), copies.plan(right, right, x_peer[3]))

    @pl.when(k == 0)
    def _():
        fwd2.wait_recv()
        kv0a.wait_recv()

    @pl.when(k == 1)
    def _():
        kv2.wait_recv()
        fwd0.wait_recv()

    transpose_kv(384, 512)
    transpose_kv(1024, 1536)

    coef = factor * math.log2(math.e)

    def attend(hp, b):
        win = pl.ds(pl.multiple_of(128 + QB * b, 128), WIN)
        rows = pl.ds(pl.multiple_of(QB * b, QB), QB)
        at_a = pl.ds(pl.multiple_of(2 * hp * HD, HD), HD)
        at_b = pl.ds(pl.multiple_of((2 * hp + 1) * HD, HD), HD)
        q = jnp.concatenate([q_h[2 * hp, rows, :], q_h[2 * hp + 1, rows, :]], axis=0)
        do = jnp.concatenate([do_v[rows, at_a], do_v[rows, at_b]], axis=0)
        do_t = jnp.concatenate([doT[2 * hp, :, rows], doT[2 * hp + 1, :, rows]], axis=1)
        s_f[...] = dot(kv[win, 0:HD], q, NT)
        p_f[...] = dot(kv[win, HD:], do, NT)
        tiles = [slice(t, t + TILE) for t in range(0, WIN, TILE)]
        top = None
        for r in tiles:
            mask = bias[b, r]
            score = s_f[r] + jnp.concatenate([mask, mask], axis=1)
            s_f[r] = score
            most = jnp.max(score.reshape(TILE // 8, 8, 2 * QB), axis=0)
            top = most if top is None else jnp.maximum(top, most)
        top = jnp.max(top, axis=0, keepdims=True) * coef
        total = None
        for r in tiles:
            weight = jnp.exp2(s_f[r] * coef - top)
            s_f[r] = weight
            low[r] = weight.astype(BF16)
            part = jnp.sum(weight.reshape(TILE // 8, 8, 2 * QB), axis=0)
            total = part if total is None else total + part
        inverse = 1.0 / jnp.sum(total, axis=0, keepdims=True)
        o_t = (dot(vT[:, win], low[...]) * inverse).astype(BF16)
        delta = jnp.sum(o_t.astype(F32) * do_t.astype(F32), axis=0, keepdims=True)
        o = o_t.T
        out_v[rows, at_a] = o[:QB]
        out_v[rows, at_b] = o[QB:]
        for r in tiles:
            dsc[r] = (s_f[r] * (p_f[r] - delta)).astype(BF16)
        dq = (dot(kT[:, win], dsc[...]) * (inverse * factor)).T.astype(BF16)
        joined[rows, at_a] = dq[:QB]
        joined[rows, at_b] = dq[QB:]
        q_n = (q.T.astype(F32) * inverse).astype(BF16)
        do_n = (do_t.astype(F32) * inverse).astype(BF16)
        acc[win, 0:HD] += dot(dsc[...], q_n, NT)
        acc[win, HD:] += dot(low[...], do_n, NT)

    def columns(group):
        return slice(group * 256, (group + 1) * 256)

    def share(group, rows):
        here = joined.at[rows, columns(group)]
        return (
            copies.plan(here, jz.at[0, rows, columns(group)], z_peer[1]),
            copies.plan(here, jz.at[2, rows, columns(group)], z_peer[3]),
        )

    def share_core(group):
        cols = columns(group)
        return copies.plan(joined.at[0:TOK, cols], joined.at[TOK : 2 * TOK, cols], sib)

    def share_far(group, rows):
        cols, middle = columns(group), (rows.start + rows.stop) // 2
        above, below = slice(rows.start, middle), slice(middle, rows.stop)
        return (
            copies.plan(jz.at[0, above, cols], jz.at[1, above, cols], z_peer[1]),
            copies.plan(jz.at[2, below, cols], jz.at[1, below, cols], z_peer[3]),
        )

    axes = {"y": (y, y_peer), "x": (x, x_peer)}
    order = (("y", "x"), ("y", "x"), ("x", "y"), ("y", "x"))
    pieces = ((0, slice(0, 256)), (1, slice(0, 256)), (2, slice(0, 128)), (2, slice(128, 256)))

    def product(group):
        def rows_of(i, carry):
            part = xT[pl.ds(4 * i, 4)].reshape(512, 2 * TOK)
            pb[group, i] = dot(part, joined[:, columns(group)]).reshape(4, 128, 256)
            return carry

        lax.fori_loop(0, 4, rows_of, 0)

    def term(chunk, there):
        group, cols = pieces[chunk]
        if order[chunk][0] == "y":
            return pb[group, there, :, :, cols]
        return pb[group, :, there, :, cols]

    first_moves, second_moves = [], []
    for chunk in range(4):
        buf = rings[chunk]
        one, two = axes[order[chunk][0]][1], axes[order[chunk][1]][1]
        if chunk == RING:
            first_moves.append(
                (
                    copies.plan(buf["s2"].at[0:2], buf["r2p"], one[1]),
                    copies.plan(buf["s2"].at[2:4], buf["r2m"], one[3]),
                    copies.plan(buf["sp"], buf["r1p"], one[1]),
                    copies.plan(buf["sm"], buf["r1m"], one[3]),
                )
            )
        else:
            first_moves.append(
                [copies.plan(buf["out1"].at[r - 1], buf["in1"].at[r - 1], one[r]) for r in (1, 2, 3)]
            )
        second_moves.append(
            [copies.plan(buf["out2"].at[r - 1], buf["in2"].at[r - 1], two[r]) for r in (1, 2, 3)]
        )

    def send_first(chunk):
        here, _ = axes[order[chunk][0]]
        for r in (1, 2, 3):
            rings[chunk]["out1"][r - 1] = term(chunk, (here + r) % 4).astype(BF16)
        begin(*first_moves[chunk])

    def ring_first(chunk):
        here, _ = axes[order[chunk][0]]
        buf, moves = rings[chunk], first_moves[chunk]
        buf["s2"][...] = term(chunk, (here + 2) % 4).astype(BF16)
        begin(moves[0], moves[1])

    def ring_second(chunk):
        here, _ = axes[order[chunk][0]]
        buf, moves = rings[chunk], first_moves[chunk]
        up, down = term(chunk, (here + 1) % 4), term(chunk, (here + 3) % 4)
        buf["sp"][2:4] = up[2:4].astype(BF16)
        buf["sm"][0:2] = down[0:2].astype(BF16)
        arrive(moves[0])
        buf["sp"][0:2] = (up[0:2] + buf["r2p"][...].astype(F32)).astype(BF16)
        begin(moves[2])
        arrive(moves[1])
        buf["sm"][2:4] = (down[2:4] + buf["r2m"][...].astype(F32)).astype(BF16)
        begin(moves[3])

    def send_second(chunk):
        here, _ = axes[order[chunk][0]]
        buf = rings[chunk]
        if chunk == RING:
            arrive(first_moves[chunk][2], first_moves[chunk][3])
            sent = buf["r1p"][...].astype(F32) + buf["r1m"][...].astype(F32)
        else:
            arrive(*first_moves[chunk])
            sent = sum(buf["in1"][r].astype(F32) for r in range(3))
        buf["t"][...] = term(chunk, here) + sent
        here, _ = axes[order[chunk][1]]
        for r in (1, 2, 3):
            buf["out2"][r - 1] = buf["t"][(here + r) % 4].astype(BF16)
        begin(*second_moves[chunk])

    def finish(chunk):
        here, _ = axes[order[chunk][1]]
        buf = rings[chunk]
        arrive(*second_moves[chunk])
        group, cols = pieces[chunk]
        first_col = group * 256 + cols.start
        last = buf["t"][here] + sum(buf["in2"][r].astype(F32) for r in range(3))
        wg_v[:, first_col : first_col + last.shape[1]] = last

    def own_term(group):
        rows = pl.ds(pl.multiple_of(z * 1024, 1024), 1024)
        return dot(joined[0:TOK, columns(group)], w_v[rows, columns(group)], NT)

    def far_term(group, slot):
        weights = wz[slot, :, :, :, columns(group)].reshape(1024, 256)
        return dot(jz[slot, :, columns(group)], weights, NT)

    def add(value):
        ig_acc[...] += value

    ones = lax.broadcasted_iota(jnp.int32, (1, 2 * HD), 1)
    scale = jnp.where(ones < HD, factor, 1.0)
    above, below, every = slice(0, 256), slice(256, 512), slice(0, TOK)
    near01, near00 = share(0, below), share(0, above)
    near10, near11 = share(1, above), share(1, below)
    near2 = share(2, every)
    far01, far00 = share_far(0, below), share_far(0, above)
    far10, far11 = share_far(1, above), share_far(1, below)
    far2 = share_far(2, every)
    core = [share_core(group) for group in range(3)]
    ws_got = copies.plan(wz.at[:, :, k], wz.at[:, :, k], sib)

    pair_c = copies.make(dkv_send.at[0, 0:256], dkv_sib.at[1, 128:384], sib)
    far_c = copies.make(dkv_send.at[0, 0:256], dkv_sib.at[1, 128:384], third)
    pair_a = copies.plan(dkv_send.at[1], dkv_sib.at[0], sib)
    pair_b = copies.make(dkv_send.at[0, 256:384], dkv_sib.at[1, 384:512], sib)
    far_d = copies.make(dkv_send.at[0, 256:384], dkv_sib.at[1, 384:512], third)
    near_d = copies.plan(dkv_send.at[2], dkv_x, prv)

    def step(i, carry):
        attend(i // 2, ((i + 1) // 2 + 1) % 2)

        @pl.when(i == 0)
        def _():
            begin(*near01)

            @pl.when(k == 0)
            def _():
                kv0b.wait_recv()

            transpose_kv(128, 384)

        @pl.when(i == 1)
        def _():
            begin(*near00, core[0])
            arrive(*near01)
            begin(*far01)
            ig_acc[...] = own_term(0)
            arrive(x_got, core[0])
            product(0)
            send_first(0)
            arrive(*wx_got)
            begin(*wx_far)

        @pl.when(i == 2)
        def _():
            begin(*near10)
            dkv_send[0, 0:256] = (acc[128:384] * scale).astype(BF16)

            @pl.when(k == 1)
            def _():
                pair_c.start()

            @pl.when(k == 0)
            def _():
                far_c.start()

            arrive(*near00)
            begin(*far00)
            arrive(*wy_got, *wx_far)
            begin(ws_got)

        return carry

    lax.fori_loop(0, 4, step, 0)
    begin(*near11, core[1])
    dkv_send[0, 256:384] = (acc[384:512] * scale).astype(BF16)
    dkv_send[1] = (acc[1024:1536] * scale).astype(BF16)
    begin(pair_a)

    @pl.when(k == 1)
    def _():
        pair_b.start()

    @pl.when(k == 0)
    def _():
        far_d.start()

    store(out_v, out_ref)
    arrive(*near10)
    begin(*far10)
    add(own_term(1))
    arrive(pair_a)

    @pl.when(k == 0)
    def _():
        pair_b.wait_recv()
        pair_c.wait_recv()

    came = dkv_sib[1 - k].astype(F32)
    dkv_send[2] = (acc[512:1024] * scale + came).astype(BF16)
    begin(near_d)
    arrive(core[1])
    product(1)
    ring_first(1)
    arrive(ws_got)
    add(far_term(0, 0))
    add(far_term(0, 2))
    arrive(*near11)
    begin(*far11)
    arrive(*far00, *far01)
    add(far_term(0, 1))
    arrive(near_d)

    @pl.when(k == 1)
    def _():
        far_c.wait_recv()
        far_d.wait_recv()

    total = acc[1536:2048] * scale + dkv_x[...].astype(F32)
    joined[0:TOK, 512:768] = (total + dkv_sib[k].astype(F32)).astype(BF16)
    begin(*near2, core[2])
    ring_second(1)
    add(own_term(2))
    arrive(core[2])
    product(2)
    send_first(2)
    send_first(3)
    send_second(0)
    add(far_term(1, 0))
    add(far_term(1, 2))
    arrive(*far10, *far11)
    add(far_term(1, 1))
    arrive(*near2)
    begin(*far2)
    add(far_term(2, 0))
    add(far_term(2, 2))
    send_second(1)
    send_second(2)
    send_second(3)
    finish(0)
    arrive(*far2)
    ig_v[...] = (ig_acc[...] + far_term(2, 1)).astype(BF16)
    store(ig_v, ig_ref)
    finish(1)
    store(wg_v.at[:, 0:512], wqg_ref)
    finish(2)
    store(wg_v.at[:, 512:640], wkg_ref)
    finish(3)
    store(wg_v.at[:, 640:768], wvg_ref)

    for copy in copies.sent:
        copy.wait_send()

    @pl.when(k == 0)
    def _():
        kv2.wait_send()
        fwd0.wait_send()
        far_c.wait_send()
        far_d.wait_send()

    @pl.when(k == 1)
    def _():
        kv0a.wait_send()
        kv0b.wait_send()
        fwd2.wait_send()
        pair_b.wait_send()
        pair_c.wait_send()

    for move in stores:
        move.wait()


def hand_over(*refs):
    sources, targets, held, sem = refs[:5], refs[5:10], refs[10:15], refs[15]
    reads = [pltpu.make_async_copy(sources[i], held[i], sem.at[0, i]) for i in range(5)]
    writes = [pltpu.make_async_copy(held[i], targets[i], sem.at[1, i]) for i in range(5)]
    for read in reads:
        read.start()
    for read, write in zip(reads, writes):
        read.wait()
        write.start()
    for write in writes:
        write.wait()


def body(inputs, query_weight, key_weight, value_weight, out_grad, doc_lengths):
    any_space = pl.BlockSpec(memory_space=pl.ANY)
    shapes = (
        jax.ShapeDtypeStruct((TOK, 512), BF16),
        jax.ShapeDtypeStruct((TOK, 1024), BF16),
        jax.ShapeDtypeStruct((128, 512), F32),
        jax.ShapeDtypeStruct((128, 128), F32),
        jax.ShapeDtypeStruct((128, 128), F32),
    )
    results = pl.pallas_call(
        kernel,
        out_shape=shapes,
        in_specs=[pl.BlockSpec(memory_space=pltpu.SMEM)] + [any_space] * 5,
        out_specs=(any_space,) * 5,
        scratch_shapes=[
            pltpu.VMEM((TOK, D), BF16),
            pltpu.VMEM((D, COLS), BF16),
            pltpu.VMEM((TOK, 512), BF16),
            pltpu.VMEM((2048, 256), BF16),
            pltpu.VMEM((HD, 2048), BF16),
            pltpu.VMEM((HD, 2048), BF16),
            pltpu.VMEM((GROUP, TOK, HD), BF16),
            pltpu.VMEM((GROUP, HD, TOK), BF16),
            pltpu.VMEM((2048, 256), F32),
            pltpu.VMEM((2, WIN, QB), F32),
            pltpu.VMEM((16, 128, 2 * TOK), BF16),
            pltpu.VMEM((16, 128, TOK), BF16),
            pltpu.VMEM((3, 4, 2, 128, COLS), BF16),
            pltpu.VMEM((2 * TOK, COLS), BF16),
            pltpu.VMEM((3, TOK, COLS), BF16),
            pltpu.VMEM((3, TOK, 256), BF16),
            pltpu.VMEM((2, TOK, 256), BF16),
            pltpu.VMEM((TOK, 256), BF16),
            [sum_scratch(w, chunk == RING) for chunk, w in enumerate((256, 256, 128, 128))],
            pltpu.VMEM((3, 4, 4, 128, 256), F32),
            pltpu.VMEM((TOK, 1024), F32),
            pltpu.VMEM((128, COLS), F32),
            pltpu.VMEM((WIN, 2 * QB), F32),
            pltpu.VMEM((WIN, 2 * QB), F32),
            pltpu.VMEM((WIN, 2 * QB), BF16),
            pltpu.VMEM((WIN, 2 * QB), BF16),
            pltpu.SemaphoreType.DMA((N_COPIES,)),
            pltpu.SemaphoreType.DMA((N_COPIES,)),
            pltpu.SemaphoreType.DMA((5,)),
            pltpu.SemaphoreType.DMA((5,)),
        ],
        compiler_params=pltpu.CompilerParams(
            collective_id=0, has_side_effects=True, vmem_limit_bytes=63 * 2**20
        ),
        cost_estimate=pl.CostEstimate(
            flops=2 * 10**10, bytes_accessed=13 * 10**6, transcendentals=4 * 10**6
        ),
        name="attention_layer",
    )(doc_lengths, inputs, query_weight, key_weight, value_weight, out_grad)
    return pl.pallas_call(
        hand_over,
        out_shape=shapes,
        in_specs=[any_space] * 5,
        out_specs=(any_space,) * 5,
        scratch_shapes=[pltpu.VMEM(shape.shape, shape.dtype) for shape in shapes]
        + [pltpu.SemaphoreType.DMA((2, 5))],
        compiler_params=pltpu.CompilerParams(vmem_limit_bytes=63 * 2**20),
        name="hand_over",
    )(*results)


def solution(mesh):
    return jax.shard_map(
        body,
        mesh=mesh,
        in_specs=(
            P("ctx", None),
            P(None, "head"),
            P(None, "head"),
            P(None, "head"),
            P("ctx", "head"),
            P(),
        ),
        out_specs=(P("ctx", "head"),) * 5,
        check_vma=False,
    )
```

```python
import functools
import math

import jax
import jax.numpy as jnp
from jax import lax
from jax.experimental import pallas as pl
from jax.experimental.pallas import tpu as pltpu
from jax.sharding import PartitionSpec as P

HD = 128
GROUP = 4
TOK = 512
D = 4096
QB = 256
WIN = 1664
COLS = 768
NEG = -1e30
MESH = pl.DeviceIdType.MESH
F32 = jnp.float32
BF16 = jnp.bfloat16

NN = (((1,), (0,)), ((), ()))
NT = (((1,), (1,)), ((), ()))


def dot(a, b, dims=NN):
    return lax.dot_general(a, b, dims, preferred_element_type=F32)


class Copies:
    def __init__(self, send_sem, recv_sem):
        self.send_sem, self.recv_sem, self.used = send_sem, recv_sem, 0
        self.sent = []

    def make(self, src, dst, device):
        idx = self.used
        self.used += 1
        return pltpu.make_async_remote_copy(
            src_ref=src,
            dst_ref=dst,
            send_sem=self.send_sem.at[idx],
            recv_sem=self.recv_sem.at[idx],
            device_id=device,
            device_id_type=MESH,
        )

    def plan(self, src, dst, device):
        copy = self.make(src, dst, device)
        self.sent.append(copy)
        return copy

    def start(self, src, dst, device):
        copy = self.plan(src, dst, device)
        copy.start()
        return copy


N_COPIES = 100
TILE = 64
RINGS = (2, 3)


def sum_scratch(width, ring):
    whole = pltpu.VMEM((4, 128, width), BF16)
    if ring:
        refs = {"r2": whole, "r1p": whole, "r1m": whole, "s2": whole, "sp": whole, "sm": whole}
    else:
        blocks = pltpu.VMEM((3, 4, 128, width), BF16)
        refs = {"out1": blocks, "in1": blocks}
    rows = pltpu.VMEM((3, 128, width), BF16)
    return refs | {"out2": rows, "in2": rows, "t": pltpu.VMEM((4, 128, width), F32)}


def kernel(
    doc_ref, x_hbm, wq_hbm, wk_hbm, wv_hbm, do_hbm,
    out_ref, ig_ref, wqg_ref, wkg_ref, wvg_ref,
    x_v, w_v, do_v, kv, kT, vT, q_h, doT, acc, bias, xT, xTo, wz, joined, jz,
    dkv_send, dkv_sib, dkv_x, rings, pb, ig_acc, wg_v, s_f, p_f, low, dsc,
    send_sem, recv_sem, load_sem, store_sem,
):
    ctx = lax.axis_index("ctx")
    z = lax.axis_index("head")
    chip = ctx // 2
    k = ctx % 2
    y, x = chip // 4, chip % 4
    factor = HD ** -0.5

    def at(yy, xx, kk, zz):
        return ((yy % 4) * 8 + (xx % 4) * 2 + kk, zz % 4)

    def chip_at(pp, kk):
        return ((pp % 16) * 2 + kk, z)

    sib = at(y, x, 1 - k, z)
    z_peer = [None] + [at(y, x, k, z + r) for r in (1, 2, 3)]
    y_peer = [None] + [at(y + r, x, k, z) for r in (1, 2, 3)]
    x_peer = [None] + [at(y, x + r, k, z) for r in (1, 2, 3)]
    nxt, prv = chip_at(chip + 1, k), chip_at(chip + 15, k)
    third = chip_at(jnp.where(k == 1, chip + 2, chip + 14), 1 - k)

    loads = [
        pltpu.make_async_copy(wk_hbm, w_v.at[:, 512:640], load_sem.at[0]),
        pltpu.make_async_copy(wv_hbm, w_v.at[:, 640:768], load_sem.at[1]),
        pltpu.make_async_copy(x_hbm, x_v, load_sem.at[2]),
        pltpu.make_async_copy(wq_hbm, w_v.at[:, 0:512], load_sem.at[3]),
        pltpu.make_async_copy(do_hbm, do_v, load_sem.at[4]),
    ]
    for load in loads:
        load.start()

    barrier = pltpu.get_barrier_semaphore()
    partners = [sib, *z_peer[1:], *y_peer[1:], *x_peer[1:], nxt, prv, third]
    for partner in partners:
        pl.semaphore_signal(barrier, inc=1, device_id=partner, device_id_type=MESH)

    ig_v, out_v = x_v.at[:, 0:1024], x_v.at[:, 1024:1536]
    copies = Copies(send_sem, recv_sem)
    stores = []

    def store(src, dst):
        move = pltpu.make_async_copy(src, dst, store_sem.at[len(stores)])
        move.start()
        stores.append(move)

    for load in loads[:3]:
        load.wait()
    kv[1536:2048, :] = dot(x_v[...], w_v[:, 512:768]).astype(BF16)
    pl.semaphore_wait(barrier, len(partners))
    own_kv = kv.at[1536:2048]
    kv1 = copies.start(own_kv, kv.at[512:1024], nxt)
    kv2 = copies.make(own_kv, kv.at[1024:1536], sib)
    kv0a = copies.make(kv.at[1920:2048], kv.at[384:512], third)
    kv0b = copies.make(kv.at[1664:1920], kv.at[128:384], third)

    @pl.when(k == 0)
    def _():
        kv2.start()

    @pl.when(k == 1)
    def _():
        kv0a.start()

    def begin(*group):
        for copy in group:
            copy.start()

    def arrive(*group):
        for copy in group:
            copy.wait_recv()

    for load in loads[3:]:
        load.wait()

    wz_got = []
    for r in (1, 2, 3):
        for begins, rows, part in ((0, 64, y), (64, 64, x)):
            first_row = pl.multiple_of(((z + r) % 4) * 1024 + part * 256 + k * 128 + begins, 64)
            there = wz.at[r - 1, part, k, begins : begins + rows]
            wz_got.append(copies.start(w_v.at[pl.ds(first_row, rows), :], there, z_peer[r]))

    for h in range(0, GROUP, 2):
        both = dot(x_v[...], w_v[:, h * HD : (h + 2) * HD]).astype(BF16)
        q_h[h] = both[:, :HD]
        q_h[h + 1] = both[:, HD:]

    def transpose_x(i, carry):
        own = pl.multiple_of((2 * i + k) * 128, 128)
        other = pl.multiple_of((2 * i + 1 - k) * 128, 128)
        xT[i, :, 0:TOK] = x_v[:, pl.ds(own, 128)].T
        xTo[i] = x_v[:, pl.ds(other, 128)].T
        return carry

    lax.fori_loop(0, 16, transpose_x, 0)
    x_got = copies.start(xTo, xT.at[:, :, TOK : 2 * TOK], sib)

    for h in range(GROUP):
        doT[h] = do_v[:, h * HD : (h + 1) * HD].T

    pos = ctx * TOK + lax.broadcasted_iota(jnp.int32, (1, TOK), 1)
    start = jnp.zeros((1, TOK), jnp.int32)
    end = jnp.int32(0)
    for j in range(32):
        length = doc_ref[j]
        end = end + length
        start = start + jnp.where(pos >= end, length, 0)
    first = start - (ctx - 3) * TOK
    for b in range(2):
        key_pos = 128 + QB * b + lax.broadcasted_iota(jnp.int32, (WIN, QB), 0)
        query_pos = 1536 + QB * b + lax.broadcasted_iota(jnp.int32, (WIN, QB), 1)
        seen = (key_pos >= first[:, b * QB : (b + 1) * QB]) & (key_pos <= query_pos)
        bias[b] = jnp.where(seen, 0.0, NEG)
    acc[...] = jnp.zeros_like(acc)
    dkv_sib[1, 0:128] = jnp.zeros((128, 256), BF16)

    def transpose_kv(begin, stop):
        kT[:, begin:stop] = kv[begin:stop, 0:HD].T
        vT[:, begin:stop] = kv[begin:stop, HD:].T

    transpose_kv(1536, 2048)
    kv1.wait_recv()
    fwd2 = copies.make(kv.at[512:1024], kv.at[1024:1536], sib)
    fwd0 = copies.make(kv.at[640:1024], kv.at[128:512], sib)

    @pl.when(k == 0)
    def _():
        fwd0.start()

    @pl.when(k == 1)
    def _():
        fwd2.start()
        kv0b.start()

    transpose_kv(512, 1024)

    arrive(*wz_got)
    w_near, w_far = [], []
    for begins, part, peer in ((0, y, y_peer), (64, x, x_peer)):
        mine = wz.at[:, part, k, begins : begins + 64]
        w_near += [copies.start(mine, mine, peer[r]) for r in (1, 3)]
        down = wz.at[:, (part + 3) % 4, k, begins : begins + 32]
        up = wz.at[:, (part + 1) % 4, k, begins + 32 : begins + 64]
        w_far += [copies.plan(down, down, peer[1]), copies.plan(up, up, peer[3])]

    @pl.when(k == 0)
    def _():
        fwd2.wait_recv()
        kv0a.wait_recv()

    @pl.when(k == 1)
    def _():
        kv2.wait_recv()
        fwd0.wait_recv()

    transpose_kv(384, 512)
    transpose_kv(1024, 1536)

    coef = factor * math.log2(math.e)

    def attend(hp, b):
        win = pl.ds(pl.multiple_of(128 + QB * b, 128), WIN)
        rows = pl.ds(pl.multiple_of(QB * b, QB), QB)
        at_a = pl.ds(pl.multiple_of(2 * hp * HD, HD), HD)
        at_b = pl.ds(pl.multiple_of((2 * hp + 1) * HD, HD), HD)
        q = jnp.concatenate([q_h[2 * hp, rows, :], q_h[2 * hp + 1, rows, :]], axis=0)
        do = jnp.concatenate([do_v[rows, at_a], do_v[rows, at_b]], axis=0)
        do_t = jnp.concatenate([doT[2 * hp, :, rows], doT[2 * hp + 1, :, rows]], axis=1)
        s_f[...] = dot(kv[win, 0:HD], q, NT)
        p_f[...] = dot(kv[win, HD:], do, NT)
        tiles = [slice(t, t + TILE) for t in range(0, WIN, TILE)]
        top = None
        for r in tiles:
            mask = bias[b, r]
            score = s_f[r] + jnp.concatenate([mask, mask], axis=1)
            s_f[r] = score
            most = jnp.max(score.reshape(TILE // 8, 8, 2 * QB), axis=0)
            top = most if top is None else jnp.maximum(top, most)
        top = jnp.max(top, axis=0, keepdims=True) * coef
        total = None
        for r in tiles:
            weight = jnp.exp2(s_f[r] * coef - top)
            s_f[r] = weight
            low[r] = weight.astype(BF16)
            part = jnp.sum(weight.reshape(TILE // 8, 8, 2 * QB), axis=0)
            total = part if total is None else total + part
        inverse = 1.0 / jnp.sum(total, axis=0, keepdims=True)
        o_t = (dot(vT[:, win], low[...]) * inverse).astype(BF16)
        delta = jnp.sum(o_t.astype(F32) * do_t.astype(F32), axis=0, keepdims=True)
        o = o_t.T
        out_v[rows, at_a] = o[:QB]
        out_v[rows, at_b] = o[QB:]
        for r in tiles:
            dsc[r] = (s_f[r] * (p_f[r] - delta)).astype(BF16)
        dq = (dot(kT[:, win], dsc[...]) * (inverse * factor)).T.astype(BF16)
        joined[rows, at_a] = dq[:QB]
        joined[rows, at_b] = dq[QB:]
        q_n = (q.T.astype(F32) * inverse).astype(BF16)
        do_n = (do_t.astype(F32) * inverse).astype(BF16)
        acc[win, 0:HD] += dot(dsc[...], q_n, NT)
        acc[win, HD:] += dot(low[...], do_n, NT)

    def columns(group):
        return slice(group * 256, (group + 1) * 256)

    def share(group, rows):
        here = joined.at[rows, columns(group)]
        return (
            copies.plan(here, jz.at[0, rows, columns(group)], z_peer[1]),
            copies.plan(here, jz.at[2, rows, columns(group)], z_peer[3]),
        )

    def share_core(group):
        cols = columns(group)
        return copies.plan(joined.at[0:TOK, cols], joined.at[TOK : 2 * TOK, cols], sib)

    def share_far(group, rows):
        cols, middle = columns(group), (rows.start + rows.stop) // 2
        above, below = slice(rows.start, middle), slice(middle, rows.stop)
        return (
            copies.plan(jz.at[0, above, cols], jz.at[1, above, cols], z_peer[1]),
            copies.plan(jz.at[2, below, cols], jz.at[1, below, cols], z_peer[3]),
        )

    axes = {"y": (y, y_peer), "x": (x, x_peer)}
    order = (("x", "y"), ("y", "x")) * 3
    pieces = [(chunk // 2, slice(chunk % 2 * 128, (chunk % 2 + 1) * 128)) for chunk in range(6)]

    def product_half(group, begins):
        def rows_of(i, carry):
            part = xT[pl.ds(4 * i, 4), :, begins : begins + TOK].reshape(512, TOK)
            whole = dot(part, joined[begins : begins + TOK, columns(group)]).reshape(4, 128, 256)
            pb[group, i] = whole if begins == 0 else pb[group, i] + whole
            return carry

        lax.fori_loop(0, 4, rows_of, 0)

    def product(group):
        def rows_of(i, carry):
            part = xT[pl.ds(4 * i, 4)].reshape(512, 2 * TOK)
            pb[group, i] = dot(part, joined[:, columns(group)]).reshape(4, 128, 256)
            return carry

        lax.fori_loop(0, 4, rows_of, 0)

    def term(chunk, there):
        group, cols = pieces[chunk]
        if order[chunk][0] == "y":
            return pb[group, there, :, :, cols]
        return pb[group, :, there, :, cols]

    first_moves, second_moves = [], []
    for chunk in range(6):
        buf = rings[chunk]
        one, two = axes[order[chunk][0]][1], axes[order[chunk][1]][1]
        if chunk in RINGS:
            first_moves.append(
                (
                    copies.plan(buf["s2"], buf["r2"], one[1]),
                    copies.plan(buf["sp"], buf["r1p"], one[1]),
                    copies.plan(buf["sm"], buf["r1m"], one[3]),
                )
            )
        else:
            first_moves.append(
                [copies.plan(buf["out1"].at[r - 1], buf["in1"].at[r - 1], one[r]) for r in (1, 2, 3)]
            )
        second_moves.append(
            [copies.plan(buf["out2"].at[r - 1], buf["in2"].at[r - 1], two[r]) for r in (1, 2, 3)]
        )

    def send_first(chunk):
        here, _ = axes[order[chunk][0]]
        for r in (1, 2, 3):
            rings[chunk]["out1"][r - 1] = term(chunk, (here + r) % 4).astype(BF16)
        begin(*first_moves[chunk])

    def ring_first(chunk):
        here, _ = axes[order[chunk][0]]
        buf = rings[chunk]
        buf["s2"][...] = term(chunk, (here + 2) % 4).astype(BF16)
        begin(first_moves[chunk][0])
        buf["sm"][...] = term(chunk, (here + 3) % 4).astype(BF16)

    def ring_down(chunk):
        begin(first_moves[chunk][2])

    def ring_up(chunk):
        here, _ = axes[order[chunk][0]]
        buf = rings[chunk]
        up = term(chunk, (here + 1) % 4)
        arrive(first_moves[chunk][0])
        buf["sp"][...] = (up + buf["r2"][...].astype(F32)).astype(BF16)
        begin(first_moves[chunk][1])

    def send_second(chunk):
        here, _ = axes[order[chunk][0]]
        buf = rings[chunk]
        if chunk in RINGS:
            arrive(first_moves[chunk][1], first_moves[chunk][2])
            sent = buf["r1p"][...].astype(F32) + buf["r1m"][...].astype(F32)
        else:
            arrive(*first_moves[chunk])
            sent = sum(buf["in1"][r].astype(F32) for r in range(3))
        buf["t"][...] = term(chunk, here) + sent
        here, _ = axes[order[chunk][1]]
        for r in (1, 2, 3):
            buf["out2"][r - 1] = buf["t"][(here + r) % 4].astype(BF16)
        begin(*second_moves[chunk])

    def finish(chunk):
        here, _ = axes[order[chunk][1]]
        buf = rings[chunk]
        arrive(*second_moves[chunk])
        group, cols = pieces[chunk]
        first_col = group * 256 + cols.start
        last = buf["t"][here] + sum(buf["in2"][r].astype(F32) for r in range(3))
        wg_v[:, first_col : first_col + last.shape[1]] = last

    def own_term(group):
        rows = pl.ds(pl.multiple_of(z * 1024, 1024), 1024)
        return dot(joined[0:TOK, columns(group)], w_v[rows, columns(group)], NT)

    def far_term(group, slot):
        weights = wz[slot, :, :, :, columns(group)].reshape(1024, 256)
        return dot(jz[slot, :, columns(group)], weights, NT)

    def add(value):
        ig_acc[...] += value

    ones = lax.broadcasted_iota(jnp.int32, (1, 2 * HD), 1)
    scale = jnp.where(ones < HD, factor, 1.0)
    above, below, every = slice(0, 256), slice(256, 512), slice(0, TOK)
    near01, near00 = share(0, below), share(0, above)
    near10, near11 = share(1, above), share(1, below)
    near2 = share(2, every)
    far01, far00 = share_far(0, below), share_far(0, above)
    far10, far11 = share_far(1, above), share_far(1, below)
    far2 = share_far(2, every)
    core = [share_core(group) for group in range(3)]
    ws_got = copies.plan(wz.at[:, :, k], wz.at[:, :, k], sib)

    pair_c = copies.make(dkv_send.at[0, 0:256], dkv_sib.at[1, 128:384], sib)
    far_c = copies.make(dkv_send.at[0, 0:256], dkv_sib.at[1, 128:384], third)
    pair_a = copies.plan(dkv_send.at[1], dkv_sib.at[0], sib)
    pair_b = copies.make(dkv_send.at[0, 256:384], dkv_sib.at[1, 384:512], sib)
    far_d = copies.make(dkv_send.at[0, 256:384], dkv_sib.at[1, 384:512], third)
    near_d = copies.plan(dkv_send.at[2], dkv_x, prv)

    def step(i, carry):
        attend(i // 2, ((i + 1) // 2 + 1) % 2)

        @pl.when(i == 0)
        def _():
            begin(*near01)

            @pl.when(k == 0)
            def _():
                kv0b.wait_recv()

            transpose_kv(128, 384)

        @pl.when(i == 1)
        def _():
            begin(*near00, core[0])
            arrive(*near01)
            begin(*far01)
            ig_acc[...] = own_term(0)
            arrive(*w_near)
            begin(*w_far)
            arrive(x_got, core[0])
            product(0)
            send_first(0)
            send_first(1)

        @pl.when(i == 2)
        def _():
            begin(*near10)
            dkv_send[0, 0:256] = (acc[128:384] * scale).astype(BF16)

            @pl.when(k == 1)
            def _():
                pair_c.start()

            @pl.when(k == 0)
            def _():
                far_c.start()

            arrive(*near00)
            begin(*far00)

        return carry

    lax.fori_loop(0, 4, step, 0)
    dkv_send[1] = (acc[1024:1536] * scale).astype(BF16)
    begin(pair_a)
    dkv_send[0, 256:384] = (acc[384:512] * scale).astype(BF16)

    @pl.when(k == 1)
    def _():
        pair_b.start()

    @pl.when(k == 0)
    def _():
        far_d.start()

    begin(*near11, core[1])
    add(own_term(1))
    arrive(pair_a)

    @pl.when(k == 0)
    def _():
        pair_b.wait_recv()
        pair_c.wait_recv()

    came = dkv_sib[1 - k].astype(F32)
    dkv_send[2] = (acc[512:1024] * scale + came).astype(BF16)
    begin(near_d)
    store(out_v, out_ref)
    arrive(*near10)
    begin(*far10)
    arrive(core[1])
    product(1)
    ring_first(2)
    ring_first(3)
    send_second(0)
    send_second(1)
    arrive(*near11)
    begin(*far11)
    arrive(*w_far)
    begin(ws_got)
    ring_up(2)
    ring_up(3)
    arrive(near_d)

    @pl.when(k == 1)
    def _():
        far_c.wait_recv()
        far_d.wait_recv()

    total = acc[1536:2048] * scale + dkv_x[...].astype(F32)
    joined[0:TOK, 512:768] = (total + dkv_sib[k].astype(F32)).astype(BF16)
    begin(core[2], *near2)
    ring_down(2)
    ring_down(3)
    product_half(2, 0)
    arrive(core[2])
    product_half(2, TOK)
    send_first(4)
    send_first(5)
    add(own_term(2))
    arrive(ws_got)
    add(far_term(0, 0))
    add(far_term(0, 2))
    send_second(2)
    send_second(3)
    arrive(*far00, *far01)
    add(far_term(0, 1))
    add(far_term(1, 0))
    arrive(*near2)
    begin(*far2)
    add(far_term(1, 2))
    arrive(*far10, *far11)
    add(far_term(1, 1))
    add(far_term(2, 0))
    add(far_term(2, 2))
    finish(0)
    finish(1)
    send_second(4)
    send_second(5)
    finish(2)
    finish(3)
    store(wg_v.at[:, 0:512], wqg_ref)
    arrive(*far2)
    ig_v[...] = (ig_acc[...] + far_term(2, 1)).astype(BF16)
    store(ig_v, ig_ref)
    finish(4)
    store(wg_v.at[:, 512:640], wkg_ref)
    finish(5)
    store(wg_v.at[:, 640:768], wvg_ref)

    for copy in copies.sent:
        copy.wait_send()

    @pl.when(k == 0)
    def _():
        kv2.wait_send()
        fwd0.wait_send()
        far_c.wait_send()
        far_d.wait_send()

    @pl.when(k == 1)
    def _():
        kv0a.wait_send()
        kv0b.wait_send()
        fwd2.wait_send()
        pair_b.wait_send()
        pair_c.wait_send()

    for move in stores:
        move.wait()


def hand_over(*refs):
    sources, targets, held, sem = refs[:5], refs[5:10], refs[10:15], refs[15]
    reads = [pltpu.make_async_copy(sources[i], held[i], sem.at[0, i]) for i in range(5)]
    writes = [pltpu.make_async_copy(held[i], targets[i], sem.at[1, i]) for i in range(5)]
    for read in reads:
        read.start()
    for read, write in zip(reads, writes):
        read.wait()
        write.start()
    for write in writes:
        write.wait()


def body(inputs, query_weight, key_weight, value_weight, out_grad, doc_lengths):
    any_space = pl.BlockSpec(memory_space=pl.ANY)
    shapes = (
        jax.ShapeDtypeStruct((TOK, 512), BF16),
        jax.ShapeDtypeStruct((TOK, 1024), BF16),
        jax.ShapeDtypeStruct((128, 512), F32),
        jax.ShapeDtypeStruct((128, 128), F32),
        jax.ShapeDtypeStruct((128, 128), F32),
    )
    results = pl.pallas_call(
        kernel,
        out_shape=shapes,
        in_specs=[pl.BlockSpec(memory_space=pltpu.SMEM)] + [any_space] * 5,
        out_specs=(any_space,) * 5,
        scratch_shapes=[
            pltpu.VMEM((TOK, D), BF16),
            pltpu.VMEM((D, COLS), BF16),
            pltpu.VMEM((TOK, 512), BF16),
            pltpu.VMEM((2048, 256), BF16),
            pltpu.VMEM((HD, 2048), BF16),
            pltpu.VMEM((HD, 2048), BF16),
            pltpu.VMEM((GROUP, TOK, HD), BF16),
            pltpu.VMEM((GROUP, HD, TOK), BF16),
            pltpu.VMEM((2048, 256), F32),
            pltpu.VMEM((2, WIN, QB), F32),
            pltpu.VMEM((16, 128, 2 * TOK), BF16),
            pltpu.VMEM((16, 128, TOK), BF16),
            pltpu.VMEM((3, 4, 2, 128, COLS), BF16),
            pltpu.VMEM((2 * TOK, COLS), BF16),
            pltpu.VMEM((3, TOK, COLS), BF16),
            pltpu.VMEM((3, TOK, 256), BF16),
            pltpu.VMEM((2, TOK, 256), BF16),
            pltpu.VMEM((TOK, 256), BF16),
            [sum_scratch(128, chunk in RINGS) for chunk in range(6)],
            pltpu.VMEM((3, 4, 4, 128, 256), F32),
            pltpu.VMEM((TOK, 1024), F32),
            pltpu.VMEM((128, COLS), F32),
            pltpu.VMEM((WIN, 2 * QB), F32),
            pltpu.VMEM((WIN, 2 * QB), F32),
            pltpu.VMEM((WIN, 2 * QB), BF16),
            pltpu.VMEM((WIN, 2 * QB), BF16),
            pltpu.SemaphoreType.DMA((N_COPIES,)),
            pltpu.SemaphoreType.DMA((N_COPIES,)),
            pltpu.SemaphoreType.DMA((5,)),
            pltpu.SemaphoreType.DMA((5,)),
        ],
        compiler_params=pltpu.CompilerParams(
            collective_id=0, has_side_effects=True, vmem_limit_bytes=63 * 2**20
        ),
        cost_estimate=pl.CostEstimate(
            flops=2 * 10**10, bytes_accessed=13 * 10**6, transcendentals=4 * 10**6
        ),
        name="attention_layer",
    )(doc_lengths, inputs, query_weight, key_weight, value_weight, out_grad)
    return pl.pallas_call(
        hand_over,
        out_shape=shapes,
        in_specs=[any_space] * 5,
        out_specs=(any_space,) * 5,
        scratch_shapes=[pltpu.VMEM(shape.shape, shape.dtype) for shape in shapes]
        + [pltpu.SemaphoreType.DMA((2, 5))],
        compiler_params=pltpu.CompilerParams(vmem_limit_bytes=63 * 2**20),
        name="hand_over",
    )(*results)


def solution(mesh):
    return jax.shard_map(
        body,
        mesh=mesh,
        in_specs=(
            P("ctx", None),
            P(None, "head"),
            P(None, "head"),
            P(None, "head"),
            P("ctx", "head"),
            P(),
        ),
        out_specs=(P("ctx", "head"),) * 5,
        check_vma=False,
    )
```

```python
import functools
import math

import jax
import jax.numpy as jnp
from jax import lax
from jax.experimental import pallas as pl
from jax.experimental.pallas import tpu as pltpu
from jax.sharding import PartitionSpec as P

HD = 128
GROUP = 4
TOK = 512
D = 4096
QB = 256
WIN = 1664
COLS = 768
NEG = -1e30
MESH = pl.DeviceIdType.MESH
F32 = jnp.float32
BF16 = jnp.bfloat16

NN = (((1,), (0,)), ((), ()))
NT = (((1,), (1,)), ((), ()))


def dot(a, b, dims=NN):
    return lax.dot_general(a, b, dims, preferred_element_type=F32)


class Copies:
    def __init__(self, send_sem, recv_sem):
        self.send_sem, self.recv_sem, self.used = send_sem, recv_sem, 0
        self.sent = []

    def make(self, src, dst, device):
        idx = self.used
        self.used += 1
        return pltpu.make_async_remote_copy(
            src_ref=src,
            dst_ref=dst,
            send_sem=self.send_sem.at[idx],
            recv_sem=self.recv_sem.at[idx],
            device_id=device,
            device_id_type=MESH,
        )

    def plan(self, src, dst, device):
        copy = self.make(src, dst, device)
        self.sent.append(copy)
        return copy

    def start(self, src, dst, device):
        copy = self.plan(src, dst, device)
        copy.start()
        return copy


N_COPIES = 100
TILE = 64
RINGS = (2, 3)


def sum_scratch(width, ring):
    whole = pltpu.VMEM((4, 128, width), BF16)
    if ring:
        refs = {"r2": whole, "r1p": whole, "r1m": whole, "s2": whole, "sp": whole, "sm": whole}
    else:
        blocks = pltpu.VMEM((3, 4, 128, width), BF16)
        refs = {"out1": blocks, "in1": blocks}
    rows = pltpu.VMEM((3, 128, width), BF16)
    return refs | {"out2": rows, "in2": rows, "t": pltpu.VMEM((4, 128, width), F32)}


def kernel(
    doc_ref, x_hbm, wq_hbm, wk_hbm, wv_hbm, do_hbm,
    out_ref, ig_ref, wqg_ref, wkg_ref, wvg_ref,
    x_v, w_v, do_v, kv, kT, vT, q_h, doT, acc, bias, xT, xTo, wz, joined, jz,
    dkv_send, dkv_sib, dkv_x, rings, pb, ig_acc, wg_v, s_f, p_f, low, dsc,
    send_sem, recv_sem, load_sem, store_sem,
):
    ctx = lax.axis_index("ctx")
    z = lax.axis_index("head")
    chip = ctx // 2
    k = ctx % 2
    y, x = chip // 4, chip % 4
    factor = HD ** -0.5

    def at(yy, xx, kk, zz):
        return ((yy % 4) * 8 + (xx % 4) * 2 + kk, zz % 4)

    def chip_at(pp, kk):
        return ((pp % 16) * 2 + kk, z)

    sib = at(y, x, 1 - k, z)
    z_peer = [None] + [at(y, x, k, z + r) for r in (1, 2, 3)]
    y_peer = [None] + [at(y + r, x, k, z) for r in (1, 2, 3)]
    x_peer = [None] + [at(y, x + r, k, z) for r in (1, 2, 3)]
    nxt, prv = chip_at(chip + 1, k), chip_at(chip + 15, k)
    third = chip_at(jnp.where(k == 1, chip + 2, chip + 14), 1 - k)

    loads = [
        pltpu.make_async_copy(wk_hbm, w_v.at[:, 512:640], load_sem.at[0]),
        pltpu.make_async_copy(wv_hbm, w_v.at[:, 640:768], load_sem.at[1]),
        pltpu.make_async_copy(x_hbm, x_v, load_sem.at[2]),
        pltpu.make_async_copy(wq_hbm, w_v.at[:, 0:512], load_sem.at[3]),
        pltpu.make_async_copy(do_hbm, do_v, load_sem.at[4]),
    ]
    for load in loads:
        load.start()

    barrier = pltpu.get_barrier_semaphore()
    partners = [sib, *z_peer[1:], *y_peer[1:], *x_peer[1:], nxt, prv, third]
    for partner in partners:
        pl.semaphore_signal(barrier, inc=1, device_id=partner, device_id_type=MESH)

    ig_v, out_v = x_v.at[:, 0:1024], x_v.at[:, 1024:1536]
    copies = Copies(send_sem, recv_sem)
    stores = []

    def store(src, dst):
        move = pltpu.make_async_copy(src, dst, store_sem.at[len(stores)])
        stores.append(move)
        return move

    out_store = store(out_v, out_ref)
    ig_store = [store(ig_v, ig_ref)]
    q_store = store(wg_v.at[:, 0:512], wqg_ref)
    kv_store = [store(wg_v.at[:, 512:640], wkg_ref), store(wg_v.at[:, 640:768], wvg_ref)]

    for load in loads[:3]:
        load.wait()
    kv[1536:2048, :] = dot(x_v[...], w_v[:, 512:768]).astype(BF16)
    pl.semaphore_wait(barrier, len(partners))
    own_kv = kv.at[1536:2048]
    kv1 = copies.make(own_kv, kv.at[512:1024], nxt)
    kv2 = copies.make(own_kv, kv.at[1024:1536], sib)
    kv0a = copies.make(kv.at[1920:2048], kv.at[384:512], third)
    kv0b = copies.make(kv.at[1664:1920], kv.at[128:384], third)

    has_prv, has_nxt = chip >= 1, chip <= 14
    gets_third, gives_third = (k == 0) & (chip >= 2), (k == 1) & (chip <= 13)

    @pl.when(has_nxt)
    def _():
        kv1.start()

    @pl.when(k == 0)
    def _():
        kv2.start()

    @pl.when(gives_third)
    def _():
        kv0a.start()

    @pl.when(jnp.logical_not(has_prv))
    def _():
        kv[512:1024, :] = jnp.zeros((512, 256), BF16)

    @pl.when((k == 0) & (chip <= 1))
    def _():
        kv[128:512, :] = jnp.zeros((384, 256), BF16)

    def begin(*group):
        for copy in group:
            copy.start()

    def arrive(*group):
        for copy in group:
            copy.wait_recv()

    for load in loads[3:]:
        load.wait()

    wz_got = []
    for r in (1, 2, 3):
        for begins, rows, part in ((0, 64, y), (64, 64, x)):
            first_row = pl.multiple_of(((z + r) % 4) * 1024 + part * 256 + k * 128 + begins, 64)
            there = wz.at[r - 1, part, k, begins : begins + rows]
            wz_got.append(copies.start(w_v.at[pl.ds(first_row, rows), :], there, z_peer[r]))

    for h in range(0, GROUP, 2):
        both = dot(x_v[...], w_v[:, h * HD : (h + 2) * HD]).astype(BF16)
        q_h[h] = both[:, :HD]
        q_h[h + 1] = both[:, HD:]

    def transpose_x(i, carry):
        own = pl.multiple_of((2 * i + k) * 128, 128)
        other = pl.multiple_of((2 * i + 1 - k) * 128, 128)
        xT[i, :, 0:TOK] = x_v[:, pl.ds(own, 128)].T
        xTo[i] = x_v[:, pl.ds(other, 128)].T
        return carry

    lax.fori_loop(0, 16, transpose_x, 0)
    x_got = copies.start(xTo, xT.at[:, :, TOK : 2 * TOK], sib)

    for h in range(GROUP):
        doT[h] = do_v[:, h * HD : (h + 1) * HD].T

    pos = ctx * TOK + lax.broadcasted_iota(jnp.int32, (1, TOK), 1)
    start = jnp.zeros((1, TOK), jnp.int32)
    end = jnp.int32(0)
    for j in range(32):
        length = doc_ref[j]
        end = end + length
        start = start + jnp.where(pos >= end, length, 0)
    first = start - (ctx - 3) * TOK
    for b in range(2):
        key_pos = 128 + QB * b + lax.broadcasted_iota(jnp.int32, (WIN, QB), 0)
        query_pos = 1536 + QB * b + lax.broadcasted_iota(jnp.int32, (WIN, QB), 1)
        seen = (key_pos >= first[:, b * QB : (b + 1) * QB]) & (key_pos <= query_pos)
        bias[b] = jnp.where(seen, 0.0, NEG)
    acc[...] = jnp.zeros_like(acc)
    dkv_sib[1, 0:128] = jnp.zeros((128, 256), BF16)

    @pl.when((k == 1) & (chip >= 14))
    def _():
        dkv_sib[1, 128:512] = jnp.zeros((384, 256), BF16)

    @pl.when(jnp.logical_not(has_nxt))
    def _():
        dkv_x[...] = jnp.zeros((TOK, 256), BF16)

    def transpose_kv(begin, stop):
        kT[:, begin:stop] = kv[begin:stop, 0:HD].T
        vT[:, begin:stop] = kv[begin:stop, HD:].T

    transpose_kv(1536, 2048)

    @pl.when(has_prv)
    def _():
        kv1.wait_recv()

    fwd2 = copies.make(kv.at[512:1024], kv.at[1024:1536], sib)
    fwd0 = copies.make(kv.at[640:1024], kv.at[128:512], sib)

    @pl.when(k == 0)
    def _():
        fwd0.start()

    @pl.when(k == 1)
    def _():
        fwd2.start()

    @pl.when(gives_third)
    def _():
        kv0b.start()

    transpose_kv(512, 1024)

    arrive(*wz_got)
    w_near, w_far = [], []
    for begins, part, peer in ((0, y, y_peer), (64, x, x_peer)):
        mine = wz.at[:, part, k, begins : begins + 64]
        w_near += [copies.start(mine, mine, peer[r]) for r in (1, 3)]
        down = wz.at[:, (part + 3) % 4, k, begins : begins + 32]
        up = wz.at[:, (part + 1) % 4, k, begins + 32 : begins + 64]
        w_far += [copies.plan(down, down, peer[1]), copies.plan(up, up, peer[3])]

    @pl.when(k == 0)
    def _():
        fwd2.wait_recv()

    @pl.when(gets_third)
    def _():
        kv0a.wait_recv()

    @pl.when(k == 1)
    def _():
        kv2.wait_recv()
        fwd0.wait_recv()

    transpose_kv(384, 512)
    transpose_kv(1024, 1536)

    coef = factor * math.log2(math.e)

    def attend(hp, b):
        win = pl.ds(pl.multiple_of(128 + QB * b, 128), WIN)
        rows = pl.ds(pl.multiple_of(QB * b, QB), QB)
        at_a = pl.ds(pl.multiple_of(2 * hp * HD, HD), HD)
        at_b = pl.ds(pl.multiple_of((2 * hp + 1) * HD, HD), HD)
        q = jnp.concatenate([q_h[2 * hp, rows, :], q_h[2 * hp + 1, rows, :]], axis=0)
        do = jnp.concatenate([do_v[rows, at_a], do_v[rows, at_b]], axis=0)
        do_t = jnp.concatenate([doT[2 * hp, :, rows], doT[2 * hp + 1, :, rows]], axis=1)
        s_f[...] = dot(kv[win, 0:HD], q, NT)
        p_f[...] = dot(kv[win, HD:], do, NT)
        tiles = [slice(t, t + TILE) for t in range(0, WIN, TILE)]
        top = None
        for r in tiles:
            mask = bias[b, r]
            score = s_f[r] + jnp.concatenate([mask, mask], axis=1)
            s_f[r] = score
            most = jnp.max(score.reshape(TILE // 8, 8, 2 * QB), axis=0)
            top = most if top is None else jnp.maximum(top, most)
        top = jnp.max(top, axis=0, keepdims=True) * coef
        total = None
        for r in tiles:
            weight = jnp.exp2(s_f[r] * coef - top)
            s_f[r] = weight
            low[r] = weight.astype(BF16)
            part = jnp.sum(weight.reshape(TILE // 8, 8, 2 * QB), axis=0)
            total = part if total is None else total + part
        inverse = 1.0 / jnp.sum(total, axis=0, keepdims=True)
        o_t = (dot(vT[:, win], low[...]) * inverse).astype(BF16)
        delta = jnp.sum(o_t.astype(F32) * do_t.astype(F32), axis=0, keepdims=True)
        o = o_t.T
        out_v[rows, at_a] = o[:QB]
        out_v[rows, at_b] = o[QB:]
        for r in tiles:
            dsc[r] = (s_f[r] * (p_f[r] - delta)).astype(BF16)
        dq = (dot(kT[:, win], dsc[...]) * (inverse * factor)).T.astype(BF16)
        joined[rows, at_a] = dq[:QB]
        joined[rows, at_b] = dq[QB:]
        q_n = (q.T.astype(F32) * inverse).astype(BF16)
        do_n = (do_t.astype(F32) * inverse).astype(BF16)
        acc[win, 0:HD] += dot(dsc[...], q_n, NT)
        acc[win, HD:] += dot(low[...], do_n, NT)

    def columns(group):
        return slice(group * 256, (group + 1) * 256)

    def share(group, rows):
        here = joined.at[rows, columns(group)]
        return (
            copies.plan(here, jz.at[0, rows, columns(group)], z_peer[1]),
            copies.plan(here, jz.at[2, rows, columns(group)], z_peer[3]),
        )

    def share_core(group):
        cols = columns(group)
        return copies.plan(joined.at[0:TOK, cols], joined.at[TOK : 2 * TOK, cols], sib)

    def share_far(group, rows):
        cols, middle = columns(group), (rows.start + rows.stop) // 2
        above, below = slice(rows.start, middle), slice(middle, rows.stop)
        return (
            copies.plan(jz.at[0, above, cols], jz.at[1, above, cols], z_peer[1]),
            copies.plan(jz.at[2, below, cols], jz.at[1, below, cols], z_peer[3]),
        )

    axes = {"y": (y, y_peer), "x": (x, x_peer)}
    order = (("x", "y"), ("y", "x")) * 3
    pieces = [(chunk // 2, slice(chunk % 2 * 128, (chunk % 2 + 1) * 128)) for chunk in range(6)]

    def product_half(group, begins):
        def rows_of(i, carry):
            part = xT[pl.ds(4 * i, 4), :, begins : begins + TOK].reshape(512, TOK)
            whole = dot(part, joined[begins : begins + TOK, columns(group)]).reshape(4, 128, 256)
            pb[group, i] = whole if begins == 0 else pb[group, i] + whole
            return carry

        lax.fori_loop(0, 4, rows_of, 0)

    def product(group):
        def rows_of(i, carry):
            part = xT[pl.ds(4 * i, 4)].reshape(512, 2 * TOK)
            pb[group, i] = dot(part, joined[:, columns(group)]).reshape(4, 128, 256)
            return carry

        lax.fori_loop(0, 4, rows_of, 0)

    def term(chunk, there):
        group, cols = pieces[chunk]
        if order[chunk][0] == "y":
            return pb[group, there, :, :, cols]
        return pb[group, :, there, :, cols]

    first_moves, second_moves = [], []
    for chunk in range(6):
        buf = rings[chunk]
        one, two = axes[order[chunk][0]][1], axes[order[chunk][1]][1]
        if chunk in RINGS:
            first_moves.append(
                (
                    copies.plan(buf["s2"], buf["r2"], one[1]),
                    copies.plan(buf["sp"], buf["r1p"], one[1]),
                    copies.plan(buf["sm"], buf["r1m"], one[3]),
                )
            )
        else:
            first_moves.append(
                [copies.plan(buf["out1"].at[r - 1], buf["in1"].at[r - 1], one[r]) for r in (1, 2, 3)]
            )
        second_moves.append(
            [copies.plan(buf["out2"].at[r - 1], buf["in2"].at[r - 1], two[r]) for r in (1, 2, 3)]
        )

    def send_first(chunk):
        here, _ = axes[order[chunk][0]]
        for r in (1, 2, 3):
            rings[chunk]["out1"][r - 1] = term(chunk, (here + r) % 4).astype(BF16)
        begin(*first_moves[chunk])

    def ring_first(chunk):
        here, _ = axes[order[chunk][0]]
        buf = rings[chunk]
        buf["s2"][...] = term(chunk, (here + 2) % 4).astype(BF16)
        begin(first_moves[chunk][0])
        buf["sm"][...] = term(chunk, (here + 3) % 4).astype(BF16)

    def ring_down(chunk):
        begin(first_moves[chunk][2])

    def ring_up(chunk):
        here, _ = axes[order[chunk][0]]
        buf = rings[chunk]
        up = term(chunk, (here + 1) % 4)
        arrive(first_moves[chunk][0])
        buf["sp"][...] = (up + buf["r2"][...].astype(F32)).astype(BF16)
        begin(first_moves[chunk][1])

    def send_second(chunk):
        here, _ = axes[order[chunk][0]]
        buf = rings[chunk]
        if chunk in RINGS:
            arrive(first_moves[chunk][1], first_moves[chunk][2])
            sent = buf["r1p"][...].astype(F32) + buf["r1m"][...].astype(F32)
        else:
            arrive(*first_moves[chunk])
            sent = sum(buf["in1"][r].astype(F32) for r in range(3))
        buf["t"][...] = term(chunk, here) + sent
        here, _ = axes[order[chunk][1]]
        for r in (1, 2, 3):
            buf["out2"][r - 1] = buf["t"][(here + r) % 4].astype(BF16)
        begin(*second_moves[chunk])

    def finish(chunk):
        here, _ = axes[order[chunk][1]]
        buf = rings[chunk]
        arrive(*second_moves[chunk])
        group, cols = pieces[chunk]
        first_col = group * 256 + cols.start
        last = buf["t"][here] + sum(buf["in2"][r].astype(F32) for r in range(3))
        wg_v[:, first_col : first_col + last.shape[1]] = last

    def own_term(group):
        rows = pl.ds(pl.multiple_of(z * 1024, 1024), 1024)
        return dot(joined[0:TOK, columns(group)], w_v[rows, columns(group)], NT)

    def far_term(group, slot):
        weights = wz[slot, :, :, :, columns(group)].reshape(1024, 256)
        return dot(jz[slot, :, columns(group)], weights, NT)

    def add(value):
        ig_acc[...] += value

    ones = lax.broadcasted_iota(jnp.int32, (1, 2 * HD), 1)
    scale = jnp.where(ones < HD, factor, 1.0)
    above, below, every = slice(0, 256), slice(256, 512), slice(0, TOK)
    near01, near00 = share(0, below), share(0, above)
    near10, near11 = share(1, above), share(1, below)
    near2 = share(2, every)
    far01, far00 = share_far(0, below), share_far(0, above)
    far10, far11 = share_far(1, above), share_far(1, below)
    far2 = share_far(2, every)
    core = [share_core(group) for group in range(3)]
    ws_got = copies.plan(wz.at[:, :, k], wz.at[:, :, k], sib)

    pair_c = copies.make(dkv_send.at[0, 0:256], dkv_sib.at[1, 128:384], sib)
    far_c = copies.make(dkv_send.at[0, 0:256], dkv_sib.at[1, 128:384], third)
    pair_a = copies.plan(dkv_send.at[1], dkv_sib.at[0], sib)
    pair_b = copies.make(dkv_send.at[0, 256:384], dkv_sib.at[1, 384:512], sib)
    far_d = copies.make(dkv_send.at[0, 256:384], dkv_sib.at[1, 384:512], third)
    near_d = copies.make(dkv_send.at[2], dkv_x, prv)

    def step(i, carry):
        attend(i // 2, ((i + 1) // 2 + 1) % 2)

        @pl.when(i == 0)
        def _():
            begin(*near01)

            @pl.when(gets_third)
            def _():
                kv0b.wait_recv()

            transpose_kv(128, 384)

        @pl.when(i == 1)
        def _():
            begin(*near00, core[0])
            arrive(*near01)
            begin(*far01)
            arrive(*w_near)
            begin(*w_far)
            arrive(x_got, core[0])
            whole = dot(xT[...].reshape(2048, 2 * TOK), joined[:, columns(0)])
            pb[0] = whole.reshape(4, 4, 128, 256)
            send_first(0)
            send_first(1)

        @pl.when(i == 2)
        def _():
            begin(*near10)
            dkv_send[0, 0:256] = (acc[128:384] * scale).astype(BF16)

            @pl.when(k == 1)
            def _():
                pair_c.start()

            @pl.when(gets_third)
            def _():
                far_c.start()

            arrive(*near00)
            begin(*far00)

        return carry

    lax.fori_loop(0, 4, step, 0)
    dkv_send[1] = (acc[1024:1536] * scale).astype(BF16)
    begin(pair_a)
    dkv_send[0, 256:384] = (acc[384:512] * scale).astype(BF16)

    @pl.when(k == 1)
    def _():
        pair_b.start()

    @pl.when(gets_third)
    def _():
        far_d.start()

    begin(*near11, core[1])
    ig_acc[...] = own_term(0)
    arrive(pair_a)

    @pl.when(k == 0)
    def _():
        pair_b.wait_recv()
        pair_c.wait_recv()

    came = dkv_sib[1 - k].astype(F32)
    dkv_send[2] = (acc[512:1024] * scale + came).astype(BF16)

    @pl.when(has_prv)
    def _():
        near_d.start()

    begin(out_store)
    arrive(*near10)
    begin(*far10)
    arrive(core[1])
    product(1)
    ring_first(2)
    ring_first(3)
    add(own_term(1))
    arrive(*near11)
    begin(*far11)
    arrive(*w_far)
    begin(ws_got)
    ring_up(2)
    ring_up(3)
    send_second(0)
    send_second(1)

    @pl.when(has_nxt)
    def _():
        near_d.wait_recv()

    @pl.when(gives_third)
    def _():
        far_c.wait_recv()
        far_d.wait_recv()

    total = acc[1536:2048] * scale + dkv_x[...].astype(F32)
    joined[0:TOK, 512:768] = (total + dkv_sib[k].astype(F32)).astype(BF16)
    begin(core[2], *near2)
    ring_down(2)
    ring_down(3)
    product_half(2, 0)
    arrive(core[2])
    product_half(2, TOK)
    send_first(4)
    send_first(5)
    add(own_term(2))
    arrive(ws_got)
    add(far_term(0, 0))
    add(far_term(0, 2))
    arrive(*far00, *far01)
    add(far_term(0, 1))
    add(far_term(1, 0))
    arrive(*near2)
    begin(*far2)
    add(far_term(1, 2))
    arrive(*far10, *far11)
    add(far_term(1, 1))
    add(far_term(2, 0))
    add(far_term(2, 2))
    finish(0)
    finish(1)
    send_second(4)
    send_second(5)
    send_second(2)
    send_second(3)
    arrive(*far2)
    ig_v[...] = (ig_acc[...] + far_term(2, 1)).astype(BF16)
    begin(*ig_store)
    finish(4)
    finish(5)
    begin(*kv_store)
    finish(2)
    finish(3)
    begin(q_store)

    for copy in copies.sent:
        copy.wait_send()

    @pl.when(has_nxt)
    def _():
        kv1.wait_send()

    @pl.when(has_prv)
    def _():
        near_d.wait_send()

    @pl.when(k == 0)
    def _():
        kv2.wait_send()
        fwd0.wait_send()

    @pl.when(k == 1)
    def _():
        fwd2.wait_send()
        pair_b.wait_send()
        pair_c.wait_send()

    @pl.when(gets_third)
    def _():
        far_c.wait_send()
        far_d.wait_send()

    @pl.when(gives_third)
    def _():
        kv0a.wait_send()
        kv0b.wait_send()

    for move in stores:
        move.wait()


def hand_over(*refs):
    sources, targets, held, sem = refs[:5], refs[5:10], refs[10:15], refs[15]
    parts = [(i, slice(r, r + 128)) for i in range(5) for r in range(0, held[i].shape[0], 128)]
    reads = [
        pltpu.make_async_copy(sources[i].at[rows], held[i].at[rows], sem.at[0, n])
        for n, (i, rows) in enumerate(parts)
    ]
    writes = [
        pltpu.make_async_copy(held[i].at[rows], targets[i].at[rows], sem.at[1, n])
        for n, (i, rows) in enumerate(parts)
    ]
    for read in reads:
        read.start()
    for read, write in zip(reads, writes):
        read.wait()
        write.start()
    for write in writes:
        write.wait()


def body(inputs, query_weight, key_weight, value_weight, out_grad, doc_lengths):
    any_space = pl.BlockSpec(memory_space=pl.ANY)
    shapes = (
        jax.ShapeDtypeStruct((TOK, 512), BF16),
        jax.ShapeDtypeStruct((TOK, 1024), BF16),
        jax.ShapeDtypeStruct((128, 512), F32),
        jax.ShapeDtypeStruct((128, 128), F32),
        jax.ShapeDtypeStruct((128, 128), F32),
    )
    results = pl.pallas_call(
        kernel,
        out_shape=shapes,
        in_specs=[pl.BlockSpec(memory_space=pltpu.SMEM)] + [any_space] * 5,
        out_specs=(any_space,) * 5,
        scratch_shapes=[
            pltpu.VMEM((TOK, D), BF16),
            pltpu.VMEM((D, COLS), BF16),
            pltpu.VMEM((TOK, 512), BF16),
            pltpu.VMEM((2048, 256), BF16),
            pltpu.VMEM((HD, 2048), BF16),
            pltpu.VMEM((HD, 2048), BF16),
            pltpu.VMEM((GROUP, TOK, HD), BF16),
            pltpu.VMEM((GROUP, HD, TOK), BF16),
            pltpu.VMEM((2048, 256), F32),
            pltpu.VMEM((2, WIN, QB), F32),
            pltpu.VMEM((16, 128, 2 * TOK), BF16),
            pltpu.VMEM((16, 128, TOK), BF16),
            pltpu.VMEM((3, 4, 2, 128, COLS), BF16),
            pltpu.VMEM((2 * TOK, COLS), BF16),
            pltpu.VMEM((3, TOK, COLS), BF16),
            pltpu.VMEM((3, TOK, 256), BF16),
            pltpu.VMEM((2, TOK, 256), BF16),
            pltpu.VMEM((TOK, 256), BF16),
            [sum_scratch(128, chunk in RINGS) for chunk in range(6)],
            pltpu.VMEM((3, 4, 4, 128, 256), F32),
            pltpu.VMEM((TOK, 1024), F32),
            pltpu.VMEM((128, COLS), F32),
            pltpu.VMEM((WIN, 2 * QB), F32),
            pltpu.VMEM((WIN, 2 * QB), F32),
            pltpu.VMEM((WIN, 2 * QB), BF16),
            pltpu.VMEM((WIN, 2 * QB), BF16),
            pltpu.SemaphoreType.DMA((N_COPIES,)),
            pltpu.SemaphoreType.DMA((N_COPIES,)),
            pltpu.SemaphoreType.DMA((5,)),
            pltpu.SemaphoreType.DMA((5,)),
        ],
        compiler_params=pltpu.CompilerParams(
            collective_id=0, has_side_effects=True, vmem_limit_bytes=63 * 2**20
        ),
        cost_estimate=pl.CostEstimate(
            flops=2 * 10**10, bytes_accessed=13 * 10**6, transcendentals=4 * 10**6
        ),
        name="attention_layer",
    )(doc_lengths, inputs, query_weight, key_weight, value_weight, out_grad)
    return pl.pallas_call(
        hand_over,
        out_shape=shapes,
        in_specs=[any_space] * 5,
        out_specs=(any_space,) * 5,
        scratch_shapes=[pltpu.VMEM(shape.shape, shape.dtype) for shape in shapes]
        + [pltpu.SemaphoreType.DMA((2, 11))],
        compiler_params=pltpu.CompilerParams(vmem_limit_bytes=63 * 2**20),
        name="hand_over",
    )(*results)


def solution(mesh):
    return jax.shard_map(
        body,
        mesh=mesh,
        in_specs=(
            P("ctx", None),
            P(None, "head"),
            P(None, "head"),
            P(None, "head"),
            P("ctx", "head"),
            P(),
        ),
        out_specs=(P("ctx", "head"),) * 5,
        check_vma=False,
    )
```

```python
import functools
import math

import jax
import jax.numpy as jnp
from jax import lax
from jax.experimental import pallas as pl
from jax.experimental.pallas import tpu as pltpu
from jax.sharding import PartitionSpec as P

HD = 128
GROUP = 4
TOK = 512
D = 4096
QB = 256
WIN = 1664
COLS = 768
NEG = -1e30
MESH = pl.DeviceIdType.MESH
F32 = jnp.float32
BF16 = jnp.bfloat16

NN = (((1,), (0,)), ((), ()))
NT = (((1,), (1,)), ((), ()))


def dot(a, b, dims=NN):
    return lax.dot_general(a, b, dims, preferred_element_type=F32)


class Copies:
    def __init__(self, send_sem, recv_sem):
        self.send_sem, self.recv_sem, self.used = send_sem, recv_sem, 0
        self.sent = []

    def make(self, src, dst, device):
        idx = self.used
        self.used += 1
        return pltpu.make_async_remote_copy(
            src_ref=src,
            dst_ref=dst,
            send_sem=self.send_sem.at[idx],
            recv_sem=self.recv_sem.at[idx],
            device_id=device,
            device_id_type=MESH,
        )

    def plan(self, src, dst, device):
        copy = self.make(src, dst, device)
        self.sent.append(copy)
        return copy

    def start(self, src, dst, device):
        copy = self.plan(src, dst, device)
        copy.start()
        return copy


N_COPIES = 120
TILE = 64
RINGS = (2, 3)


def sum_scratch(width, ring):
    whole = pltpu.VMEM((4, 128, width), BF16)
    if ring:
        refs = {"r2": whole, "r1p": whole, "r1m": whole, "s2": whole, "sp": whole, "sm": whole}
    else:
        blocks = pltpu.VMEM((3, 4, 128, width), BF16)
        refs = {"out1": blocks, "in1": blocks}
    rows = pltpu.VMEM((3, 128, width), BF16)
    return refs | {"out2": rows, "in2": rows, "t": pltpu.VMEM((4, 128, width), F32)}


def kernel(
    doc_ref, x_hbm, wq_hbm, wk_hbm, wv_hbm, do_hbm,
    out_ref, ig_ref, wqg_ref, wkg_ref, wvg_ref,
    x_v, w_v, do_v, kv, kT, vT, q_h, doT, acc, bias, xT, xTo, wz, joined, jz,
    dkv_send, dkv_sib, dkv_x, rings, pb, ig_acc, wg_v, s_f, p_f, low, dsc,
    send_sem, recv_sem, load_sem, store_sem,
):
    ctx = lax.axis_index("ctx")
    z = lax.axis_index("head")
    chip = ctx // 2
    k = ctx % 2
    y, x = chip // 4, chip % 4
    factor = HD ** -0.5

    def at(yy, xx, kk, zz):
        return ((yy % 4) * 8 + (xx % 4) * 2 + kk, zz % 4)

    def chip_at(pp, kk):
        return ((pp % 16) * 2 + kk, z)

    sib = at(y, x, 1 - k, z)
    z_peer = [None] + [at(y, x, k, z + r) for r in (1, 2, 3)]
    y_peer = [None] + [at(y + r, x, k, z) for r in (1, 2, 3)]
    x_peer = [None] + [at(y, x + r, k, z) for r in (1, 2, 3)]
    nxt, prv = chip_at(chip + 1, k), chip_at(chip + 15, k)
    third = chip_at(jnp.where(k == 1, chip + 2, chip + 14), 1 - k)

    loads = [
        pltpu.make_async_copy(wk_hbm, w_v.at[:, 512:640], load_sem.at[0]),
        pltpu.make_async_copy(wv_hbm, w_v.at[:, 640:768], load_sem.at[1]),
        pltpu.make_async_copy(x_hbm, x_v, load_sem.at[2]),
        pltpu.make_async_copy(wq_hbm, w_v.at[:, 0:512], load_sem.at[3]),
        pltpu.make_async_copy(do_hbm, do_v, load_sem.at[4]),
    ]
    for load in loads:
        load.start()

    barrier = pltpu.get_barrier_semaphore()
    partners = [sib, *z_peer[1:], *y_peer[1:], *x_peer[1:], nxt, prv, third]
    for partner in partners:
        pl.semaphore_signal(barrier, inc=1, device_id=partner, device_id_type=MESH)

    ig_v, out_v = x_v.at[:, 0:1024], x_v.at[:, 1024:1536]
    copies = Copies(send_sem, recv_sem)
    stores = []

    def store(src, dst):
        move = pltpu.make_async_copy(src, dst, store_sem.at[len(stores)])
        stores.append(move)
        return move

    out_store = store(out_v, out_ref)
    ig_store = [store(ig_v, ig_ref)]
    q_store = store(wg_v.at[:, 0:512], wqg_ref)
    kv_store = [store(wg_v.at[:, 512:640], wkg_ref), store(wg_v.at[:, 640:768], wvg_ref)]

    pl.semaphore_wait(barrier, len(partners))
    wz_got = []
    for r in (1, 2, 3):
        for begins, part in ((0, y), (64, x)):
            row = pl.multiple_of(((z + r) % 4) * 1024 + part * 256 + k * 128 + begins, 64)
            there = wz.at[r - 1, part, k, begins : begins + 64]
            for weight, cols in ((wq_hbm, slice(0, 512)), (wk_hbm, slice(512, 640)), (wv_hbm, slice(640, 768))):
                wz_got.append(copies.start(weight.at[pl.ds(row, 64), :], there.at[:, cols], z_peer[r]))

    for load in loads[:3]:
        load.wait()
    kv[1536:2048, :] = dot(x_v[...], w_v[:, 512:768]).astype(BF16)
    own_kv = kv.at[1536:2048]
    kv1 = copies.make(own_kv, kv.at[512:1024], nxt)
    kv2 = copies.make(own_kv, kv.at[1024:1536], sib)
    kv0a = copies.make(kv.at[1920:2048], kv.at[384:512], third)
    kv0b = copies.make(kv.at[1664:1920], kv.at[128:384], third)

    has_prv, has_nxt = chip >= 1, chip <= 14
    gets_third, gives_third = (k == 0) & (chip >= 2), (k == 1) & (chip <= 13)

    @pl.when(has_nxt)
    def _():
        kv1.start()

    @pl.when(k == 0)
    def _():
        kv2.start()

    @pl.when(gives_third)
    def _():
        kv0a.start()

    @pl.when(jnp.logical_not(has_prv))
    def _():
        kv[512:1024, :] = jnp.zeros((512, 256), BF16)

    @pl.when((k == 0) & (chip <= 1))
    def _():
        kv[128:512, :] = jnp.zeros((384, 256), BF16)

    def begin(*group):
        for copy in group:
            copy.start()

    def arrive(*group):
        for copy in group:
            copy.wait_recv()

    for load in loads[3:]:
        load.wait()

    for h in range(0, GROUP, 2):
        both = dot(x_v[...], w_v[:, h * HD : (h + 2) * HD]).astype(BF16)
        q_h[h] = both[:, :HD]
        q_h[h + 1] = both[:, HD:]

    def transpose_x(i, carry):
        own = pl.multiple_of((2 * i + k) * 128, 128)
        other = pl.multiple_of((2 * i + 1 - k) * 128, 128)
        xT[i, :, 0:TOK] = x_v[:, pl.ds(own, 128)].T
        xTo[i] = x_v[:, pl.ds(other, 128)].T
        return carry

    lax.fori_loop(0, 16, transpose_x, 0)
    x_got = copies.start(xTo, xT.at[:, :, TOK : 2 * TOK], sib)

    for h in range(GROUP):
        doT[h] = do_v[:, h * HD : (h + 1) * HD].T

    pos = ctx * TOK + lax.broadcasted_iota(jnp.int32, (1, TOK), 1)
    start = jnp.zeros((1, TOK), jnp.int32)
    end = jnp.int32(0)
    for j in range(32):
        length = doc_ref[j]
        end = end + length
        start = start + jnp.where(pos >= end, length, 0)
    first = start - (ctx - 3) * TOK
    for b in range(2):
        key_pos = 128 + QB * b + lax.broadcasted_iota(jnp.int32, (WIN, QB), 0)
        query_pos = 1536 + QB * b + lax.broadcasted_iota(jnp.int32, (WIN, QB), 1)
        seen = (key_pos >= first[:, b * QB : (b + 1) * QB]) & (key_pos <= query_pos)
        bias[b] = jnp.where(seen, 0.0, NEG)
    acc[...] = jnp.zeros_like(acc)
    dkv_sib[1, 0:128] = jnp.zeros((128, 256), BF16)

    @pl.when((k == 1) & (chip >= 14))
    def _():
        dkv_sib[1, 128:512] = jnp.zeros((384, 256), BF16)

    @pl.when(jnp.logical_not(has_nxt))
    def _():
        dkv_x[...] = jnp.zeros((TOK, 256), BF16)

    def transpose_kv(begin, stop):
        kT[:, begin:stop] = kv[begin:stop, 0:HD].T
        vT[:, begin:stop] = kv[begin:stop, HD:].T

    transpose_kv(1536, 2048)

    @pl.when(has_prv)
    def _():
        kv1.wait_recv()

    fwd2 = copies.make(kv.at[512:1024], kv.at[1024:1536], sib)
    fwd0 = copies.make(kv.at[640:1024], kv.at[128:512], sib)

    @pl.when(k == 0)
    def _():
        fwd0.start()

    @pl.when(k == 1)
    def _():
        fwd2.start()

    @pl.when(gives_third)
    def _():
        kv0b.start()

    transpose_kv(512, 1024)

    arrive(*wz_got)
    w_near, w_far = [], []
    for begins, part, peer in ((0, y, y_peer), (64, x, x_peer)):
        mine = wz.at[:, part, k, begins : begins + 64]
        w_near += [copies.start(mine, mine, peer[r]) for r in (1, 3)]
        down = wz.at[:, (part + 3) % 4, k, begins : begins + 32]
        up = wz.at[:, (part + 1) % 4, k, begins + 32 : begins + 64]
        w_far += [copies.plan(down, down, peer[1]), copies.plan(up, up, peer[3])]

    @pl.when(k == 0)
    def _():
        fwd2.wait_recv()

    @pl.when(gets_third)
    def _():
        kv0a.wait_recv()

    @pl.when(k == 1)
    def _():
        kv2.wait_recv()
        fwd0.wait_recv()

    transpose_kv(384, 512)
    transpose_kv(1024, 1536)

    coef = factor * math.log2(math.e)

    def attend(hp, b):
        win = pl.ds(pl.multiple_of(128 + QB * b, 128), WIN)
        rows = pl.ds(pl.multiple_of(QB * b, QB), QB)
        at_a = pl.ds(pl.multiple_of(2 * hp * HD, HD), HD)
        at_b = pl.ds(pl.multiple_of((2 * hp + 1) * HD, HD), HD)
        q = jnp.concatenate([q_h[2 * hp, rows, :], q_h[2 * hp + 1, rows, :]], axis=0)
        do = jnp.concatenate([do_v[rows, at_a], do_v[rows, at_b]], axis=0)
        do_t = jnp.concatenate([doT[2 * hp, :, rows], doT[2 * hp + 1, :, rows]], axis=1)
        s_f[...] = dot(kv[win, 0:HD], q, NT)
        p_f[...] = dot(kv[win, HD:], do, NT)
        tiles = [slice(t, t + TILE) for t in range(0, WIN, TILE)]
        top = None
        for r in tiles:
            mask = bias[b, r]
            score = s_f[r] + jnp.concatenate([mask, mask], axis=1)
            s_f[r] = score
            most = jnp.max(score.reshape(TILE // 8, 8, 2 * QB), axis=0)
            top = most if top is None else jnp.maximum(top, most)
        top = jnp.max(top, axis=0, keepdims=True) * coef
        total = None
        for r in tiles:
            weight = jnp.exp2(s_f[r] * coef - top)
            s_f[r] = weight
            low[r] = weight.astype(BF16)
            part = jnp.sum(weight.reshape(TILE // 8, 8, 2 * QB), axis=0)
            total = part if total is None else total + part
        inverse = 1.0 / jnp.sum(total, axis=0, keepdims=True)
        o_t = (dot(vT[:, win], low[...]) * inverse).astype(BF16)
        delta = jnp.sum(o_t.astype(F32) * do_t.astype(F32), axis=0, keepdims=True)
        o = o_t.T
        out_v[rows, at_a] = o[:QB]
        out_v[rows, at_b] = o[QB:]
        for r in tiles:
            dsc[r] = (s_f[r] * (p_f[r] - delta)).astype(BF16)
        dq = (dot(kT[:, win], dsc[...]) * (inverse * factor)).T.astype(BF16)
        joined[rows, at_a] = dq[:QB]
        joined[rows, at_b] = dq[QB:]
        q_n = (q.T.astype(F32) * inverse).astype(BF16)
        do_n = (do_t.astype(F32) * inverse).astype(BF16)
        acc[win, 0:HD] += dot(dsc[...], q_n, NT)
        acc[win, HD:] += dot(low[...], do_n, NT)

    def columns(group):
        return slice(group * 256, (group + 1) * 256)

    def share(group, rows):
        here = joined.at[rows, columns(group)]
        return (
            copies.plan(here, jz.at[0, rows, columns(group)], z_peer[1]),
            copies.plan(here, jz.at[2, rows, columns(group)], z_peer[3]),
        )

    def share_core(group):
        cols = columns(group)
        return copies.plan(joined.at[0:TOK, cols], joined.at[TOK : 2 * TOK, cols], sib)

    def share_far(group, rows):
        cols, middle = columns(group), (rows.start + rows.stop) // 2
        above, below = slice(rows.start, middle), slice(middle, rows.stop)
        return (
            copies.plan(jz.at[0, above, cols], jz.at[1, above, cols], z_peer[1]),
            copies.plan(jz.at[2, below, cols], jz.at[1, below, cols], z_peer[3]),
        )

    axes = {"y": (y, y_peer), "x": (x, x_peer)}
    order = (("x", "y"), ("y", "x")) * 3
    pieces = [(chunk // 2, slice(chunk % 2 * 128, (chunk % 2 + 1) * 128)) for chunk in range(6)]

    def product_half(group, begins):
        def rows_of(i, carry):
            part = xT[pl.ds(4 * i, 4), :, begins : begins + TOK].reshape(512, TOK)
            whole = dot(part, joined[begins : begins + TOK, columns(group)]).reshape(4, 128, 256)
            pb[group, i] = whole if begins == 0 else pb[group, i] + whole
            return carry

        lax.fori_loop(0, 4, rows_of, 0)

    def product(group):
        def rows_of(i, carry):
            part = xT[pl.ds(4 * i, 4)].reshape(512, 2 * TOK)
            pb[group, i] = dot(part, joined[:, columns(group)]).reshape(4, 128, 256)
            return carry

        lax.fori_loop(0, 4, rows_of, 0)

    def term(chunk, there):
        group, cols = pieces[chunk]
        if order[chunk][0] == "y":
            return pb[group, there, :, :, cols]
        return pb[group, :, there, :, cols]

    first_moves, second_moves = [], []
    for chunk in range(6):
        buf = rings[chunk]
        one, two = axes[order[chunk][0]][1], axes[order[chunk][1]][1]
        if chunk in RINGS:
            first_moves.append(
                (
                    copies.plan(buf["s2"], buf["r2"], one[1]),
                    copies.plan(buf["sp"], buf["r1p"], one[1]),
                    copies.plan(buf["sm"], buf["r1m"], one[3]),
                )
            )
        else:
            first_moves.append(
                [copies.plan(buf["out1"].at[r - 1], buf["in1"].at[r - 1], one[r]) for r in (1, 2, 3)]
            )
        second_moves.append(
            [copies.plan(buf["out2"].at[r - 1], buf["in2"].at[r - 1], two[r]) for r in (1, 2, 3)]
        )

    def send_first(chunk):
        here, _ = axes[order[chunk][0]]
        for r in (1, 2, 3):
            rings[chunk]["out1"][r - 1] = term(chunk, (here + r) % 4).astype(BF16)
        begin(*first_moves[chunk])

    def ring_first(chunk):
        here, _ = axes[order[chunk][0]]
        buf = rings[chunk]
        buf["s2"][...] = term(chunk, (here + 2) % 4).astype(BF16)
        begin(first_moves[chunk][0])
        buf["sm"][...] = term(chunk, (here + 3) % 4).astype(BF16)

    def ring_down(chunk):
        begin(first_moves[chunk][2])

    def ring_up(chunk):
        here, _ = axes[order[chunk][0]]
        buf = rings[chunk]
        up = term(chunk, (here + 1) % 4)
        arrive(first_moves[chunk][0])
        buf["sp"][...] = (up + buf["r2"][...].astype(F32)).astype(BF16)
        begin(first_moves[chunk][1])

    def send_second(chunk):
        here, _ = axes[order[chunk][0]]
        buf = rings[chunk]
        if chunk in RINGS:
            arrive(first_moves[chunk][1], first_moves[chunk][2])
            sent = buf["r1p"][...].astype(F32) + buf["r1m"][...].astype(F32)
        else:
            arrive(*first_moves[chunk])
            sent = sum(buf["in1"][r].astype(F32) for r in range(3))
        buf["t"][...] = term(chunk, here) + sent
        here, _ = axes[order[chunk][1]]
        for r in (1, 2, 3):
            buf["out2"][r - 1] = buf["t"][(here + r) % 4].astype(BF16)
        begin(*second_moves[chunk])

    def finish(chunk):
        here, _ = axes[order[chunk][1]]
        buf = rings[chunk]
        arrive(*second_moves[chunk])
        group, cols = pieces[chunk]
        first_col = group * 256 + cols.start
        last = buf["t"][here] + sum(buf["in2"][r].astype(F32) for r in range(3))
        wg_v[:, first_col : first_col + last.shape[1]] = last

    def own_term(group):
        rows = pl.ds(pl.multiple_of(z * 1024, 1024), 1024)
        return dot(joined[0:TOK, columns(group)], w_v[rows, columns(group)], NT)

    def far_term(group, slot):
        weights = wz[slot, :, :, :, columns(group)].reshape(1024, 256)
        return dot(jz[slot, :, columns(group)], weights, NT)

    def add(value):
        ig_acc[...] += value

    ones = lax.broadcasted_iota(jnp.int32, (1, 2 * HD), 1)
    scale = jnp.where(ones < HD, factor, 1.0)
    above, below, every = slice(0, 256), slice(256, 512), slice(0, TOK)
    near01, near00 = share(0, below), share(0, above)
    near10, near11 = share(1, above), share(1, below)
    near2 = share(2, every)
    far01, far00 = share_far(0, below), share_far(0, above)
    far10, far11 = share_far(1, above), share_far(1, below)
    far2 = share_far(2, every)
    core = [share_core(group) for group in range(3)]
    ws_got = copies.plan(wz.at[:, :, k], wz.at[:, :, k], sib)

    pair_c = copies.make(dkv_send.at[0, 0:256], dkv_sib.at[1, 128:384], sib)
    far_c = copies.make(dkv_send.at[0, 0:256], dkv_sib.at[1, 128:384], third)
    pair_a = copies.plan(dkv_send.at[1], dkv_sib.at[0], sib)
    pair_b = copies.make(dkv_send.at[0, 256:384], dkv_sib.at[1, 384:512], sib)
    far_d = copies.make(dkv_send.at[0, 256:384], dkv_sib.at[1, 384:512], third)
    near_d = copies.make(dkv_send.at[2], dkv_x, prv)

    def step(i, carry):
        attend(i // 2, ((i + 1) // 2 + 1) % 2)

        @pl.when(i == 0)
        def _():
            begin(*near01)

            @pl.when(gets_third)
            def _():
                kv0b.wait_recv()

            transpose_kv(128, 384)

        @pl.when(i == 1)
        def _():
            begin(*near00, core[0])
            arrive(*near01)
            begin(*far01)
            arrive(*w_near)
            begin(*w_far)
            arrive(x_got, core[0])
            whole = dot(xT[...].reshape(2048, 2 * TOK), joined[:, columns(0)])
            pb[0] = whole.reshape(4, 4, 128, 256)
            send_first(0)
            send_first(1)

        @pl.when(i == 2)
        def _():
            begin(*near10)
            dkv_send[0, 0:256] = (acc[128:384] * scale).astype(BF16)

            @pl.when(k == 1)
            def _():
                pair_c.start()

            @pl.when(gets_third)
            def _():
                far_c.start()

            arrive(*near00)
            begin(*far00)

        return carry

    lax.fori_loop(0, 4, step, 0)
    dkv_send[1] = (acc[1024:1536] * scale).astype(BF16)
    begin(pair_a)
    dkv_send[0, 256:384] = (acc[384:512] * scale).astype(BF16)

    @pl.when(k == 1)
    def _():
        pair_b.start()

    @pl.when(gets_third)
    def _():
        far_d.start()

    begin(*near11, core[1])
    ig_acc[...] = own_term(0)
    arrive(pair_a)

    @pl.when(k == 0)
    def _():
        pair_b.wait_recv()
        pair_c.wait_recv()

    came = dkv_sib[1 - k].astype(F32)
    dkv_send[2] = (acc[512:1024] * scale + came).astype(BF16)

    @pl.when(has_prv)
    def _():
        near_d.start()

    begin(out_store)
    arrive(*near10)
    begin(*far10)
    arrive(core[1])
    product(1)
    ring_first(2)
    ring_first(3)
    add(own_term(1))
    arrive(*near11)
    begin(*far11)
    arrive(*w_far)
    begin(ws_got)
    ring_up(2)
    ring_up(3)
    send_second(0)
    send_second(1)

    @pl.when(has_nxt)
    def _():
        near_d.wait_recv()

    @pl.when(gives_third)
    def _():
        far_c.wait_recv()
        far_d.wait_recv()

    total = acc[1536:2048] * scale + dkv_x[...].astype(F32)
    joined[0:TOK, 512:768] = (total + dkv_sib[k].astype(F32)).astype(BF16)
    begin(core[2], *near2)
    ring_down(2)
    ring_down(3)
    product_half(2, 0)
    arrive(core[2])
    product_half(2, TOK)
    send_first(4)
    send_first(5)
    add(own_term(2))
    arrive(ws_got)
    add(far_term(0, 0))
    add(far_term(0, 2))
    arrive(*far00, *far01)
    add(far_term(0, 1))
    add(far_term(1, 0))
    send_second(2)
    send_second(3)
    arrive(*near2)
    begin(*far2)
    add(far_term(1, 2))
    arrive(*far10, *far11)
    add(far_term(1, 1))
    add(far_term(2, 0))
    add(far_term(2, 2))
    finish(0)
    finish(1)
    send_second(4)
    send_second(5)
    arrive(*far2)
    ig_v[...] = (ig_acc[...] + far_term(2, 1)).astype(BF16)
    begin(*ig_store)
    finish(2)
    finish(3)
    begin(q_store)
    finish(4)
    finish(5)
    begin(*kv_store)

    for copy in copies.sent:
        copy.wait_send()

    @pl.when(has_nxt)
    def _():
        kv1.wait_send()

    @pl.when(has_prv)
    def _():
        near_d.wait_send()

    @pl.when(k == 0)
    def _():
        kv2.wait_send()
        fwd0.wait_send()

    @pl.when(k == 1)
    def _():
        fwd2.wait_send()
        pair_b.wait_send()
        pair_c.wait_send()

    @pl.when(gets_third)
    def _():
        far_c.wait_send()
        far_d.wait_send()

    @pl.when(gives_third)
    def _():
        kv0a.wait_send()
        kv0b.wait_send()

    for move in stores:
        move.wait()


def hand_over(*refs):
    sources, targets, held, sem = refs[:5], refs[5:10], refs[10:15], refs[15]
    parts = [(i, slice(r, r + 128)) for i in range(5) for r in range(0, held[i].shape[0], 128)]
    reads = [
        pltpu.make_async_copy(sources[i].at[rows], held[i].at[rows], sem.at[0, n])
        for n, (i, rows) in enumerate(parts)
    ]
    writes = [
        pltpu.make_async_copy(held[i].at[rows], targets[i].at[rows], sem.at[1, n])
        for n, (i, rows) in enumerate(parts)
    ]
    for read in reads:
        read.start()
    for read, write in zip(reads, writes):
        read.wait()
        write.start()
    for write in writes:
        write.wait()


def body(inputs, query_weight, key_weight, value_weight, out_grad, doc_lengths):
    any_space = pl.BlockSpec(memory_space=pl.ANY)
    shapes = (
        jax.ShapeDtypeStruct((TOK, 512), BF16),
        jax.ShapeDtypeStruct((TOK, 1024), BF16),
        jax.ShapeDtypeStruct((128, 512), F32),
        jax.ShapeDtypeStruct((128, 128), F32),
        jax.ShapeDtypeStruct((128, 128), F32),
    )
    results = pl.pallas_call(
        kernel,
        out_shape=shapes,
        in_specs=[pl.BlockSpec(memory_space=pltpu.SMEM)] + [any_space] * 5,
        out_specs=(any_space,) * 5,
        scratch_shapes=[
            pltpu.VMEM((TOK, D), BF16),
            pltpu.VMEM((D, COLS), BF16),
            pltpu.VMEM((TOK, 512), BF16),
            pltpu.VMEM((2048, 256), BF16),
            pltpu.VMEM((HD, 2048), BF16),
            pltpu.VMEM((HD, 2048), BF16),
            pltpu.VMEM((GROUP, TOK, HD), BF16),
            pltpu.VMEM((GROUP, HD, TOK), BF16),
            pltpu.VMEM((2048, 256), F32),
            pltpu.VMEM((2, WIN, QB), F32),
            pltpu.VMEM((16, 128, 2 * TOK), BF16),
            pltpu.VMEM((16, 128, TOK), BF16),
            pltpu.VMEM((3, 4, 2, 128, COLS), BF16),
            pltpu.VMEM((2 * TOK, COLS), BF16),
            pltpu.VMEM((3, TOK, COLS), BF16),
            pltpu.VMEM((3, TOK, 256), BF16),
            pltpu.VMEM((2, TOK, 256), BF16),
            pltpu.VMEM((TOK, 256), BF16),
            [sum_scratch(128, chunk in RINGS) for chunk in range(6)],
            pltpu.VMEM((3, 4, 4, 128, 256), F32),
            pltpu.VMEM((TOK, 1024), F32),
            pltpu.VMEM((128, COLS), F32),
            pltpu.VMEM((WIN, 2 * QB), F32),
            pltpu.VMEM((WIN, 2 * QB), F32),
            pltpu.VMEM((WIN, 2 * QB), BF16),
            pltpu.VMEM((WIN, 2 * QB), BF16),
            pltpu.SemaphoreType.DMA((N_COPIES,)),
            pltpu.SemaphoreType.DMA((N_COPIES,)),
            pltpu.SemaphoreType.DMA((5,)),
            pltpu.SemaphoreType.DMA((5,)),
        ],
        compiler_params=pltpu.CompilerParams(
            collective_id=0, has_side_effects=True, vmem_limit_bytes=63 * 2**20
        ),
        cost_estimate=pl.CostEstimate(
            flops=2 * 10**10, bytes_accessed=13 * 10**6, transcendentals=4 * 10**6
        ),
        name="attention_layer",
    )(doc_lengths, inputs, query_weight, key_weight, value_weight, out_grad)
    return pl.pallas_call(
        hand_over,
        out_shape=shapes,
        in_specs=[any_space] * 5,
        out_specs=(any_space,) * 5,
        scratch_shapes=[pltpu.VMEM(shape.shape, shape.dtype) for shape in shapes]
        + [pltpu.SemaphoreType.DMA((2, 11))],
        compiler_params=pltpu.CompilerParams(vmem_limit_bytes=63 * 2**20),
        name="hand_over",
    )(*results)


def solution(mesh):
    return jax.shard_map(
        body,
        mesh=mesh,
        in_specs=(
            P("ctx", None),
            P(None, "head"),
            P(None, "head"),
            P(None, "head"),
            P("ctx", "head"),
            P(),
        ),
        out_specs=(P("ctx", "head"),) * 5,
        check_vma=False,
    )
```

```python
import functools
import math

import jax
import jax.numpy as jnp
from jax import lax
from jax.experimental import pallas as pl
from jax.experimental.pallas import tpu as pltpu
from jax.sharding import PartitionSpec as P

HD = 128
GROUP = 4
TOK = 512
D = 4096
QB = 256
WIN = 1664
COLS = 768
NEG = -1e30
MESH = pl.DeviceIdType.MESH
F32 = jnp.float32
BF16 = jnp.bfloat16

NN = (((1,), (0,)), ((), ()))
NT = (((1,), (1,)), ((), ()))


def dot(a, b, dims=NN):
    return lax.dot_general(a, b, dims, preferred_element_type=F32)


class Copies:
    def __init__(self, send_sem, recv_sem):
        self.send_sem, self.recv_sem, self.used = send_sem, recv_sem, 0
        self.sent = []

    def make(self, src, dst, device):
        idx = self.used
        self.used += 1
        return pltpu.make_async_remote_copy(
            src_ref=src,
            dst_ref=dst,
            send_sem=self.send_sem.at[idx],
            recv_sem=self.recv_sem.at[idx],
            device_id=device,
            device_id_type=MESH,
        )

    def plan(self, src, dst, device):
        copy = self.make(src, dst, device)
        self.sent.append(copy)
        return copy

    def start(self, src, dst, device):
        copy = self.plan(src, dst, device)
        copy.start()
        return copy


N_COPIES = 120
TILE = 64
RINGS = (2, 3)


def sum_scratch(width, ring):
    whole = pltpu.VMEM((4, 128, width), BF16)
    if ring:
        refs = {"r2": whole, "r1p": whole, "r1m": whole, "s2": whole, "sp": whole, "sm": whole}
    else:
        blocks = pltpu.VMEM((3, 4, 128, width), BF16)
        refs = {"out1": blocks, "in1": blocks}
    rows = pltpu.VMEM((3, 128, width), BF16)
    return refs | {"out2": rows, "in2": rows, "t": pltpu.VMEM((4, 128, width), F32)}


def kernel(
    doc_ref, x_hbm, wq_hbm, wk_hbm, wv_hbm, do_hbm,
    out_ref, ig_ref, wqg_ref, wkg_ref, wvg_ref,
    x_v, w_v, do_v, kv, kT, vT, q_h, doT, acc, bias, xT, xTo, wz, joined, jz,
    dkv_send, dkv_sib, dkv_x, rings, pb, ig_acc, wg_v, s_f, p_f, low, dsc,
    send_sem, recv_sem, load_sem, store_sem,
):
    ctx = lax.axis_index("ctx")
    z = lax.axis_index("head")
    chip = ctx // 2
    k = ctx % 2
    y, x = chip // 4, chip % 4
    factor = HD ** -0.5

    def at(yy, xx, kk, zz):
        return ((yy % 4) * 8 + (xx % 4) * 2 + kk, zz % 4)

    def chip_at(pp, kk):
        return ((pp % 16) * 2 + kk, z)

    sib = at(y, x, 1 - k, z)
    z_peer = [None] + [at(y, x, k, z + r) for r in (1, 2, 3)]
    y_peer = [None] + [at(y + r, x, k, z) for r in (1, 2, 3)]
    x_peer = [None] + [at(y, x + r, k, z) for r in (1, 2, 3)]
    nxt, prv = chip_at(chip + 1, k), chip_at(chip + 15, k)
    third = chip_at(jnp.where(k == 1, chip + 2, chip + 14), 1 - k)

    loads = [
        pltpu.make_async_copy(wk_hbm, w_v.at[:, 512:640], load_sem.at[0]),
        pltpu.make_async_copy(wv_hbm, w_v.at[:, 640:768], load_sem.at[1]),
        pltpu.make_async_copy(x_hbm, x_v, load_sem.at[2]),
        pltpu.make_async_copy(wq_hbm, w_v.at[:, 0:512], load_sem.at[3]),
        pltpu.make_async_copy(do_hbm, do_v, load_sem.at[4]),
    ]
    for load in loads:
        load.start()

    barrier = pltpu.get_barrier_semaphore()
    partners = [sib, *z_peer[1:], *y_peer[1:], *x_peer[1:], nxt, prv, third]
    for partner in partners:
        pl.semaphore_signal(barrier, inc=1, device_id=partner, device_id_type=MESH)

    ig_v, out_v = x_v.at[:, 0:1024], x_v.at[:, 1024:1536]
    copies = Copies(send_sem, recv_sem)
    stores = []

    def store(src, dst):
        move = pltpu.make_async_copy(src, dst, store_sem.at[len(stores)])
        stores.append(move)
        return move

    out_store = store(out_v, out_ref)
    ig_store = [store(ig_v, ig_ref)]
    q_store = store(wg_v.at[:, 0:512], wqg_ref)
    kv_store = [store(wg_v.at[:, 512:640], wkg_ref), store(wg_v.at[:, 640:768], wvg_ref)]

    pl.semaphore_wait(barrier, len(partners))
    wz_got = []
    for r in (1, 2, 3):
        for begins, part in ((0, y), (64, x)):
            row = pl.multiple_of(((z + r) % 4) * 1024 + part * 256 + k * 128 + begins, 64)
            there = wz.at[r - 1, part, k, begins : begins + 64]
            for weight, cols in ((wq_hbm, slice(0, 512)), (wk_hbm, slice(512, 640)), (wv_hbm, slice(640, 768))):
                wz_got.append(copies.start(weight.at[pl.ds(row, 64), :], there.at[:, cols], z_peer[r]))

    for load in loads[:3]:
        load.wait()
    kv[1536:2048, :] = dot(x_v[...], w_v[:, 512:768]).astype(BF16)
    own_kv = kv.at[1536:2048]
    kv1 = copies.make(own_kv, kv.at[512:1024], nxt)
    kv2 = copies.make(own_kv, kv.at[1024:1536], sib)
    kv0a = copies.make(kv.at[1920:2048], kv.at[384:512], third)
    kv0b = copies.make(kv.at[1664:1920], kv.at[128:384], third)

    has_prv, has_nxt = chip >= 1, chip <= 14
    gets_third, gives_third = (k == 0) & (chip >= 2), (k == 1) & (chip <= 13)

    @pl.when(has_nxt)
    def _():
        kv1.start()

    @pl.when(k == 0)
    def _():
        kv2.start()

    @pl.when(gives_third)
    def _():
        kv0a.start()

    @pl.when(jnp.logical_not(has_prv))
    def _():
        kv[512:1024, :] = jnp.zeros((512, 256), BF16)

    @pl.when((k == 0) & (chip <= 1))
    def _():
        kv[128:512, :] = jnp.zeros((384, 256), BF16)

    def begin(*group):
        for copy in group:
            copy.start()

    def arrive(*group):
        for copy in group:
            copy.wait_recv()

    for load in loads[3:]:
        load.wait()

    for h in range(0, GROUP, 2):
        both = dot(x_v[...], w_v[:, h * HD : (h + 2) * HD]).astype(BF16)
        q_h[h] = both[:, :HD]
        q_h[h + 1] = both[:, HD:]

    def transpose_x(i, carry):
        own = pl.multiple_of((2 * i + k) * 128, 128)
        other = pl.multiple_of((2 * i + 1 - k) * 128, 128)
        xT[i, :, 0:TOK] = x_v[:, pl.ds(own, 128)].T
        xTo[i] = x_v[:, pl.ds(other, 128)].T
        return carry

    lax.fori_loop(0, 16, transpose_x, 0)
    x_got = copies.start(xTo, xT.at[:, :, TOK : 2 * TOK], sib)

    for h in range(GROUP):
        doT[h] = do_v[:, h * HD : (h + 1) * HD].T

    pos = ctx * TOK + lax.broadcasted_iota(jnp.int32, (1, TOK), 1)
    start = jnp.zeros((1, TOK), jnp.int32)
    end = jnp.int32(0)
    for j in range(32):
        length = doc_ref[j]
        end = end + length
        start = start + jnp.where(pos >= end, length, 0)
    first = start - (ctx - 3) * TOK
    for b in range(2):
        key_pos = 128 + QB * b + lax.broadcasted_iota(jnp.int32, (WIN, QB), 0)
        query_pos = 1536 + QB * b + lax.broadcasted_iota(jnp.int32, (WIN, QB), 1)
        seen = (key_pos >= first[:, b * QB : (b + 1) * QB]) & (key_pos <= query_pos)
        bias[b] = jnp.where(seen, 0.0, NEG)
    acc[...] = jnp.zeros_like(acc)
    dkv_sib[1, 0:128] = jnp.zeros((128, 256), BF16)

    @pl.when((k == 1) & (chip >= 14))
    def _():
        dkv_sib[1, 128:512] = jnp.zeros((384, 256), BF16)

    @pl.when(jnp.logical_not(has_nxt))
    def _():
        dkv_x[...] = jnp.zeros((TOK, 256), BF16)

    def transpose_kv(begin, stop):
        kT[:, begin:stop] = kv[begin:stop, 0:HD].T
        vT[:, begin:stop] = kv[begin:stop, HD:].T

    transpose_kv(1536, 2048)

    @pl.when(has_prv)
    def _():
        kv1.wait_recv()

    fwd2 = copies.make(kv.at[512:1024], kv.at[1024:1536], sib)
    fwd0 = copies.make(kv.at[640:1024], kv.at[128:512], sib)

    @pl.when(k == 0)
    def _():
        fwd0.start()

    @pl.when(k == 1)
    def _():
        fwd2.start()

    @pl.when(gives_third)
    def _():
        kv0b.start()

    transpose_kv(512, 1024)

    arrive(*wz_got)
    w_near, w_far = [], []
    for begins, part, peer in ((0, y, y_peer), (64, x, x_peer)):
        mine = wz.at[:, part, k, begins : begins + 64]
        w_near += [copies.start(mine, mine, peer[r]) for r in (1, 3)]
        down = wz.at[:, (part + 3) % 4, k, begins : begins + 32]
        up = wz.at[:, (part + 1) % 4, k, begins + 32 : begins + 64]
        w_far += [copies.plan(down, down, peer[1]), copies.plan(up, up, peer[3])]

    @pl.when(k == 0)
    def _():
        fwd2.wait_recv()

    @pl.when(gets_third)
    def _():
        kv0a.wait_recv()

    @pl.when(k == 1)
    def _():
        kv2.wait_recv()
        fwd0.wait_recv()

    transpose_kv(384, 512)
    transpose_kv(1024, 1536)

    coef = factor * math.log2(math.e)

    def attend(hp, b):
        win = pl.ds(pl.multiple_of(128 + QB * b, 128), WIN)
        rows = pl.ds(pl.multiple_of(QB * b, QB), QB)
        at_a = pl.ds(pl.multiple_of(2 * hp * HD, HD), HD)
        at_b = pl.ds(pl.multiple_of((2 * hp + 1) * HD, HD), HD)
        q = jnp.concatenate([q_h[2 * hp, rows, :], q_h[2 * hp + 1, rows, :]], axis=0)
        do = jnp.concatenate([do_v[rows, at_a], do_v[rows, at_b]], axis=0)
        do_t = jnp.concatenate([doT[2 * hp, :, rows], doT[2 * hp + 1, :, rows]], axis=1)
        s_f[...] = dot(kv[win, 0:HD], q, NT)
        p_f[...] = dot(kv[win, HD:], do, NT)
        tiles = [slice(t, t + TILE) for t in range(0, WIN, TILE)]
        top = None
        for r in tiles:
            mask = bias[b, r]
            score = s_f[r] + jnp.concatenate([mask, mask], axis=1)
            s_f[r] = score
            most = jnp.max(score.reshape(TILE // 8, 8, 2 * QB), axis=0)
            top = most if top is None else jnp.maximum(top, most)
        top = jnp.max(top, axis=0, keepdims=True) * coef
        total = None
        for r in tiles:
            weight = jnp.exp2(s_f[r] * coef - top)
            s_f[r] = weight
            low[r] = weight.astype(BF16)
            part = jnp.sum(weight.reshape(TILE // 8, 8, 2 * QB), axis=0)
            total = part if total is None else total + part
        inverse = 1.0 / jnp.sum(total, axis=0, keepdims=True)
        o_t = (dot(vT[:, win], low[...]) * inverse).astype(BF16)
        delta = jnp.sum(o_t.astype(F32) * do_t.astype(F32), axis=0, keepdims=True)
        o = o_t.T
        out_v[rows, at_a] = o[:QB]
        out_v[rows, at_b] = o[QB:]
        for r in tiles:
            dsc[r] = (s_f[r] * (p_f[r] - delta)).astype(BF16)
        dq = (dot(kT[:, win], dsc[...]) * (inverse * factor)).T.astype(BF16)
        joined[rows, at_a] = dq[:QB]
        joined[rows, at_b] = dq[QB:]
        q_n = (q.T.astype(F32) * inverse).astype(BF16)
        do_n = (do_t.astype(F32) * inverse).astype(BF16)
        acc[win, 0:HD] += dot(dsc[...], q_n, NT)
        acc[win, HD:] += dot(low[...], do_n, NT)

    def columns(group):
        return slice(group * 256, (group + 1) * 256)

    def share(group, rows):
        here = joined.at[rows, columns(group)]
        return (
            copies.plan(here, jz.at[0, rows, columns(group)], z_peer[1]),
            copies.plan(here, jz.at[2, rows, columns(group)], z_peer[3]),
        )

    def share_core(group):
        cols = columns(group)
        return copies.plan(joined.at[0:TOK, cols], joined.at[TOK : 2 * TOK, cols], sib)

    def share_far(group, rows):
        cols, middle = columns(group), (rows.start + rows.stop) // 2
        above, below = slice(rows.start, middle), slice(middle, rows.stop)
        return (
            copies.plan(jz.at[0, above, cols], jz.at[1, above, cols], z_peer[1]),
            copies.plan(jz.at[2, below, cols], jz.at[1, below, cols], z_peer[3]),
        )

    axes = {"y": (y, y_peer), "x": (x, x_peer)}
    order = (("x", "y"), ("y", "x")) * 3
    pieces = [(chunk // 2, slice(chunk % 2 * 128, (chunk % 2 + 1) * 128)) for chunk in range(6)]

    def product_halves(group):
        def rows_of(j, carry):
            @pl.when(j == 4)
            def _():
                core[group].wait_recv()

            block = j % 4
            toks = pl.ds(pl.multiple_of((j // 4) * TOK, TOK), TOK)
            part = xT[pl.ds(4 * block, 4), :, toks].reshape(512, TOK)
            pb[group, block] += dot(part, joined[toks, columns(group)]).reshape(4, 128, 256)
            return carry

        lax.fori_loop(0, 8, rows_of, 0)

    def product(group):
        def rows_of(i, carry):
            part = xT[pl.ds(4 * i, 4)].reshape(512, 2 * TOK)
            pb[group, i] = dot(part, joined[:, columns(group)]).reshape(4, 128, 256)
            return carry

        lax.fori_loop(0, 4, rows_of, 0)

    def term(chunk, there):
        group, cols = pieces[chunk]
        if order[chunk][0] == "y":
            return pb[group, there, :, :, cols]
        return pb[group, :, there, :, cols]

    first_moves, second_moves = [], []
    for chunk in range(6):
        buf = rings[chunk]
        one, two = axes[order[chunk][0]][1], axes[order[chunk][1]][1]
        if chunk in RINGS:
            first_moves.append(
                (
                    copies.plan(buf["s2"], buf["r2"], one[1]),
                    copies.plan(buf["sp"], buf["r1p"], one[1]),
                    copies.plan(buf["sm"], buf["r1m"], one[3]),
                )
            )
        else:
            first_moves.append(
                [copies.plan(buf["out1"].at[r - 1], buf["in1"].at[r - 1], one[r]) for r in (1, 2, 3)]
            )
        second_moves.append(
            [copies.plan(buf["out2"].at[r - 1], buf["in2"].at[r - 1], two[r]) for r in (1, 2, 3)]
        )

    def send_first(chunk):
        here, _ = axes[order[chunk][0]]
        for r in (1, 2, 3):
            rings[chunk]["out1"][r - 1] = term(chunk, (here + r) % 4).astype(BF16)
        begin(*first_moves[chunk])

    def ring_first(chunk):
        here, _ = axes[order[chunk][0]]
        buf = rings[chunk]
        buf["s2"][...] = term(chunk, (here + 2) % 4).astype(BF16)
        begin(first_moves[chunk][0])
        buf["sm"][...] = term(chunk, (here + 3) % 4).astype(BF16)

    def ring_down(chunk):
        begin(first_moves[chunk][2])

    def ring_up(chunk):
        here, _ = axes[order[chunk][0]]
        buf = rings[chunk]
        up = term(chunk, (here + 1) % 4)
        arrive(first_moves[chunk][0])
        buf["sp"][...] = (up + buf["r2"][...].astype(F32)).astype(BF16)
        begin(first_moves[chunk][1])

    def send_second(chunk):
        here, _ = axes[order[chunk][0]]
        buf = rings[chunk]
        if chunk in RINGS:
            arrive(first_moves[chunk][1], first_moves[chunk][2])
            sent = buf["r1p"][...].astype(F32) + buf["r1m"][...].astype(F32)
        else:
            arrive(*first_moves[chunk])
            sent = sum(buf["in1"][r].astype(F32) for r in range(3))
        buf["t"][...] = term(chunk, here) + sent
        here, _ = axes[order[chunk][1]]
        for r in (1, 2, 3):
            buf["out2"][r - 1] = buf["t"][(here + r) % 4].astype(BF16)
        begin(*second_moves[chunk])

    def finish(chunk):
        here, _ = axes[order[chunk][1]]
        buf = rings[chunk]
        arrive(*second_moves[chunk])
        group, cols = pieces[chunk]
        first_col = group * 256 + cols.start
        last = buf["t"][here] + sum(buf["in2"][r].astype(F32) for r in range(3))
        wg_v[:, first_col : first_col + last.shape[1]] = last

    def own_term(group):
        rows = pl.ds(pl.multiple_of(z * 1024, 1024), 1024)
        return dot(joined[0:TOK, columns(group)], w_v[rows, columns(group)], NT)

    def far_term(group, slot):
        weights = wz[slot, :, :, :, columns(group)].reshape(1024, 256)
        return dot(jz[slot, :, columns(group)], weights, NT)

    def add(value):
        ig_acc[...] += value

    ones = lax.broadcasted_iota(jnp.int32, (1, 2 * HD), 1)
    scale = jnp.where(ones < HD, factor, 1.0)
    above, below, every = slice(0, 256), slice(256, 512), slice(0, TOK)
    near01, near00 = share(0, below), share(0, above)
    near10, near11 = share(1, above), share(1, below)
    near2 = share(2, every)
    far01, far00 = share_far(0, below), share_far(0, above)
    far10, far11 = share_far(1, above), share_far(1, below)
    far2 = share_far(2, every)
    core = [share_core(group) for group in range(3)]
    ws_got = copies.plan(wz.at[:, :, k], wz.at[:, :, k], sib)

    pair_c = copies.make(dkv_send.at[0, 0:256], dkv_sib.at[1, 128:384], sib)
    far_c = copies.make(dkv_send.at[0, 0:256], dkv_sib.at[1, 128:384], third)
    pair_a = copies.plan(dkv_send.at[1], dkv_sib.at[0], sib)
    pair_b = copies.make(dkv_send.at[0, 256:384], dkv_sib.at[1, 384:512], sib)
    far_d = copies.make(dkv_send.at[0, 256:384], dkv_sib.at[1, 384:512], third)
    near_d = copies.make(dkv_send.at[2], dkv_x, prv)

    def step(i, carry):
        attend(i // 2, ((i + 1) // 2 + 1) % 2)

        @pl.when(i == 0)
        def _():
            begin(*near01)

            @pl.when(gets_third)
            def _():
                kv0b.wait_recv()

            transpose_kv(128, 384)

        @pl.when(i == 1)
        def _():
            begin(*near00, core[0])
            arrive(*near01)
            begin(*far01)
            arrive(*w_near)
            begin(*w_far)
            arrive(x_got, core[0])
            whole = dot(xT[...].reshape(2048, 2 * TOK), joined[:, columns(0)])
            pb[0] = whole.reshape(4, 4, 128, 256)
            send_first(0)
            send_first(1)

        @pl.when(i == 2)
        def _():
            begin(*near10)
            dkv_send[0, 0:256] = (acc[128:384] * scale).astype(BF16)

            @pl.when(k == 1)
            def _():
                pair_c.start()

            @pl.when(gets_third)
            def _():
                far_c.start()

            arrive(*near00)
            begin(*far00)

        return carry

    lax.fori_loop(0, 4, step, 0)
    dkv_send[1] = (acc[1024:1536] * scale).astype(BF16)
    begin(pair_a)
    dkv_send[0, 256:384] = (acc[384:512] * scale).astype(BF16)

    @pl.when(k == 1)
    def _():
        pair_b.start()

    @pl.when(gets_third)
    def _():
        far_d.start()

    begin(*near11, core[1])
    ig_acc[...] = own_term(0)
    arrive(pair_a)

    @pl.when(k == 0)
    def _():
        pair_b.wait_recv()
        pair_c.wait_recv()

    came = dkv_sib[1 - k].astype(F32)
    dkv_send[2] = (acc[512:1024] * scale + came).astype(BF16)

    @pl.when(has_prv)
    def _():
        near_d.start()

    begin(out_store)
    arrive(*near10)
    begin(*far10)
    arrive(core[1])
    product(1)
    ring_first(2)
    ring_first(3)
    add(own_term(1))
    arrive(*near11)
    begin(*far11)
    arrive(*w_far)
    begin(ws_got)
    ring_up(2)
    ring_up(3)
    send_second(0)
    send_second(1)
    pb[2] = jnp.zeros((4, 4, 128, 256), F32)

    @pl.when(has_nxt)
    def _():
        near_d.wait_recv()

    @pl.when(gives_third)
    def _():
        far_c.wait_recv()
        far_d.wait_recv()

    total = acc[1536:2048] * scale + dkv_x[...].astype(F32)
    joined[0:TOK, 512:768] = (total + dkv_sib[k].astype(F32)).astype(BF16)
    begin(core[2], *near2)
    ring_down(2)
    ring_down(3)
    product_halves(2)
    send_first(4)
    send_first(5)
    add(own_term(2))
    arrive(ws_got)
    add(far_term(0, 0))
    add(far_term(0, 2))
    arrive(*far00, *far01)
    add(far_term(0, 1))
    add(far_term(1, 0))
    send_second(2)
    send_second(3)
    arrive(*near2)
    begin(*far2)
    add(far_term(1, 2))
    arrive(*far10, *far11)
    add(far_term(1, 1))
    add(far_term(2, 0))
    add(far_term(2, 2))
    finish(0)
    finish(1)
    send_second(4)
    send_second(5)
    arrive(*far2)
    ig_v[...] = (ig_acc[...] + far_term(2, 1)).astype(BF16)
    begin(*ig_store)
    finish(2)
    finish(3)
    begin(q_store)
    finish(4)
    finish(5)
    begin(*kv_store)

    for copy in copies.sent:
        copy.wait_send()

    @pl.when(has_nxt)
    def _():
        kv1.wait_send()

    @pl.when(has_prv)
    def _():
        near_d.wait_send()

    @pl.when(k == 0)
    def _():
        kv2.wait_send()
        fwd0.wait_send()

    @pl.when(k == 1)
    def _():
        fwd2.wait_send()
        pair_b.wait_send()
        pair_c.wait_send()

    @pl.when(gets_third)
    def _():
        far_c.wait_send()
        far_d.wait_send()

    @pl.when(gives_third)
    def _():
        kv0a.wait_send()
        kv0b.wait_send()

    for move in stores:
        move.wait()


def hand_over(*refs):
    sources, targets, held, sem = refs[:5], refs[5:10], refs[10:15], refs[15]
    parts = [(i, slice(r, r + 128)) for i in range(5) for r in range(0, held[i].shape[0], 128)]
    reads = [
        pltpu.make_async_copy(sources[i].at[rows], held[i].at[rows], sem.at[0, n])
        for n, (i, rows) in enumerate(parts)
    ]
    writes = [
        pltpu.make_async_copy(held[i].at[rows], targets[i].at[rows], sem.at[1, n])
        for n, (i, rows) in enumerate(parts)
    ]
    for read in reads:
        read.start()
    for read, write in zip(reads, writes):
        read.wait()
        write.start()
    for write in writes:
        write.wait()


def body(inputs, query_weight, key_weight, value_weight, out_grad, doc_lengths):
    any_space = pl.BlockSpec(memory_space=pl.ANY)
    shapes = (
        jax.ShapeDtypeStruct((TOK, 512), BF16),
        jax.ShapeDtypeStruct((TOK, 1024), BF16),
        jax.ShapeDtypeStruct((128, 512), F32),
        jax.ShapeDtypeStruct((128, 128), F32),
        jax.ShapeDtypeStruct((128, 128), F32),
    )
    results = pl.pallas_call(
        kernel,
        out_shape=shapes,
        in_specs=[pl.BlockSpec(memory_space=pltpu.SMEM)] + [any_space] * 5,
        out_specs=(any_space,) * 5,
        scratch_shapes=[
            pltpu.VMEM((TOK, D), BF16),
            pltpu.VMEM((D, COLS), BF16),
            pltpu.VMEM((TOK, 512), BF16),
            pltpu.VMEM((2048, 256), BF16),
            pltpu.VMEM((HD, 2048), BF16),
            pltpu.VMEM((HD, 2048), BF16),
            pltpu.VMEM((GROUP, TOK, HD), BF16),
            pltpu.VMEM((GROUP, HD, TOK), BF16),
            pltpu.VMEM((2048, 256), F32),
            pltpu.VMEM((2, WIN, QB), F32),
            pltpu.VMEM((16, 128, 2 * TOK), BF16),
            pltpu.VMEM((16, 128, TOK), BF16),
            pltpu.VMEM((3, 4, 2, 128, COLS), BF16),
            pltpu.VMEM((2 * TOK, COLS), BF16),
            pltpu.VMEM((3, TOK, COLS), BF16),
            pltpu.VMEM((3, TOK, 256), BF16),
            pltpu.VMEM((2, TOK, 256), BF16),
            pltpu.VMEM((TOK, 256), BF16),
            [sum_scratch(128, chunk in RINGS) for chunk in range(6)],
            pltpu.VMEM((3, 4, 4, 128, 256), F32),
            pltpu.VMEM((TOK, 1024), F32),
            pltpu.VMEM((128, COLS), F32),
            pltpu.VMEM((WIN, 2 * QB), F32),
            pltpu.VMEM((WIN, 2 * QB), F32),
            pltpu.VMEM((WIN, 2 * QB), BF16),
            pltpu.VMEM((WIN, 2 * QB), BF16),
            pltpu.SemaphoreType.DMA((N_COPIES,)),
            pltpu.SemaphoreType.DMA((N_COPIES,)),
            pltpu.SemaphoreType.DMA((5,)),
            pltpu.SemaphoreType.DMA((5,)),
        ],
        compiler_params=pltpu.CompilerParams(
            collective_id=0, has_side_effects=True, vmem_limit_bytes=63 * 2**20
        ),
        cost_estimate=pl.CostEstimate(
            flops=2 * 10**10, bytes_accessed=13 * 10**6, transcendentals=4 * 10**6
        ),
        name="attention_layer",
    )(doc_lengths, inputs, query_weight, key_weight, value_weight, out_grad)
    return pl.pallas_call(
        hand_over,
        out_shape=shapes,
        in_specs=[any_space] * 5,
        out_specs=(any_space,) * 5,
        scratch_shapes=[pltpu.VMEM(shape.shape, shape.dtype) for shape in shapes]
        + [pltpu.SemaphoreType.DMA((2, 11))],
        compiler_params=pltpu.CompilerParams(vmem_limit_bytes=63 * 2**20),
        name="hand_over",
    )(*results)


def solution(mesh):
    return jax.shard_map(
        body,
        mesh=mesh,
        in_specs=(
            P("ctx", None),
            P(None, "head"),
            P(None, "head"),
            P(None, "head"),
            P("ctx", "head"),
            P(),
        ),
        out_specs=(P("ctx", "head"),) * 5,
        check_vma=False,
    )
```
